128 devices in a mesh: ccd: 64 (over x, z, y), strip: 2 (over core).
Axes of the slice: x: 4, y: 4, z: 4, core: 2. Of those that a mesh axis runs over, the one named last changes fastest.
Arguments:
- template: bfloat16 [16384, 8, 512], P(('ccd', 'strip')), may hold values from -8 to 8
- route_dest: int32 [16384], P(('ccd', 'strip')), may hold values from 0 to 127, as said below
- route_row: int32 [16384], P(('ccd', 'strip')), may hold values from 0 to 1016
- kern_row: bfloat16 [12, 21], replicated, may hold values from -1 to 1
- kern_col: bfloat16 [12, 21], replicated, may hold values from -1 to 1
- science: float32 [131072, 512], P(('ccd', 'strip'))
- noise_sigma: float32 [128], P(('ccd', 'strip')), may hold values from 1 to 4
- stamp_row: int32 [2048], P(('ccd', 'strip')), may hold values from 0 to 992
- stamp_col: int32 [2048], P(('ccd', 'strip')), may hold values from 0 to 480
- band_shift: int32 [128], replicated, may hold values from 0 to 63, as said below
- psf_row: bfloat16 [15], replicated, may hold values from -1.5 to 1.5
- psf_col: bfloat16 [15], replicated, may hold values from -1.5 to 1.5
Outputs:
- difference: bfloat16 [131072, 512], P(('ccd', 'strip'))
- stamp_cut: bfloat16 [2048, 1024], P(('ccd', 'strip'))
- coefficients: float32 [12], replicated
- filtered: float32 [131072, 512], P(('ccd', 'strip'))
The draws below stay inside these ranges and needn't reach their ends.
Inputs may be any that keep to these rules, and one draw needn't show every extreme that they name: `route_dest`: among the 128 pieces of one device no destination appears more than 2 times, and on every device some destination appears exactly 2 times. `band_shift`: no value appears more than 4 times, and some value appears exactly 4 times.
All inputs are finite; a program needn't handle non-finite values.
Results may differ from the reference program's by a relative error of at most 0.0065.
Values may be sent and summed in bfloat16 or wider, within the bound.
No kernel may reach another device: no remote copies, remote signals or barrier semaphores. Data moves between devices by JAX's collectives and lax.ppermute only.
A program may use at most 128 MiB of HBM per device.

```python
import jax
import jax.numpy as jnp
from jax import lax

ROWS = 1024
COLS = 512
BAND = 8
CAP = 2
BASIS = 12
STAMPS = 16
STAMP = 32
CCDS = 64
STRIPS = 2
DEVS = 128
PIECES = 128
BANDS = 128
RELAY_CAP = 4
KTAPS = 21
PSF_TAPS = 15


def kernel_pair(key):
    first_key = jax.random.fold_in(key, 11)
    second_key = jax.random.fold_in(key, 12)
    grid_shape = (BASIS, KTAPS)
    along_rows = jax.random.truncated_normal(first_key, -4.0, 4.0, grid_shape, jnp.float32)
    along_cols = jax.random.truncated_normal(second_key, -4.0, 4.0, grid_shape, jnp.float32)
    factor = KTAPS ** (-0.5)
    return ((along_rows * factor).astype(jnp.bfloat16).astype(jnp.float32), (along_cols * factor).astype(jnp.bfloat16).astype(jnp.float32))


def piece_routes(key):
    slot_count = DEVS * CAP
    slot_dest = jnp.arange(slot_count, dtype=jnp.int32) // CAP
    scores = jax.random.randint(jax.random.fold_in(key, 21), (DEVS, slot_count), 0, 2 ** 20, dtype=jnp.int32)
    popular = jax.random.randint(jax.random.fold_in(key, 22), (DEVS,), 0, 2 ** 19, dtype=jnp.int32)
    scores = scores - jnp.take(popular, slot_dest)[None, :]
    forced = jax.random.randint(jax.random.fold_in(key, 23), (DEVS, 1), 0, DEVS, dtype=jnp.int32)
    scores = jnp.where(slot_dest[None, :] == forced, -2 ** 20, scores)
    scores = scores * slot_count + jnp.arange(slot_count, dtype=jnp.int32)[None, :]
    chosen = jnp.argsort(scores, axis=1)[:, :PIECES].astype(jnp.int32)
    destinations = (chosen // CAP).astype(jnp.int32)
    shuffle_keys = jax.random.randint(jax.random.fold_in(key, 24), (DEVS, PIECES), 0, 2 ** 20, dtype=jnp.int32) * PIECES + jnp.arange(PIECES, dtype=jnp.int32)[None, :]
    mixer_order = jnp.argsort(shuffle_keys, axis=1)
    destinations = jnp.take_along_axis(destinations, mixer_order, axis=1).reshape(-1).astype(jnp.int32)
    first_rows = jax.random.randint(jax.random.fold_in(key, 25), (DEVS * PIECES,), 0, ROWS - BAND + 1, dtype=jnp.int32)
    return (destinations, first_rows)


def piece_values(key):
    value_key = jax.random.fold_in(key, 31)
    grid_shape = (DEVS * PIECES, BAND, COLS)
    values = jax.random.truncated_normal(value_key, -5.0, 5.0, grid_shape, jnp.float32)
    return jnp.clip(values, -8.0, 8.0).astype(jnp.bfloat16).astype(jnp.float32)


def sigma_values(key):
    rising = jnp.sqrt(1.0 + 2.0 * jnp.arange(DEVS, dtype=jnp.float32) / max(DEVS - 1, 1))
    upper = 0.2
    return rising * jnp.exp(jax.random.uniform(jax.random.fold_in(key, 41), (DEVS,), jnp.float32, 0.0, upper))


def shifted_sum(picture, kernel, axis_number):
    half_width = (kernel.shape[0] - 1) // 2
    padding = [(0, 0), (0, 0)]
    padding[axis_number] = (half_width, half_width)
    padded = jnp.pad(picture, padding)
    running = jnp.zeros_like(picture)
    for tap_index in range(kernel.shape[0]):
        running = running + kernel[tap_index] * lax.slice_in_dim(padded, tap_index, tap_index + picture.shape[axis_number], axis=axis_number)
    return running


def draw_template(key, part):
    return piece_values(key).astype(jnp.bfloat16)


def draw_route_dest(key, part):
    return piece_routes(key)[0].astype(jnp.int32)


def draw_route_row(key, part):
    return piece_routes(key)[1].astype(jnp.int32)


def draw_kern_row(key, part):
    return kernel_pair(key)[0].astype(jnp.bfloat16)


def draw_kern_col(key, part):
    return kernel_pair(key)[1].astype(jnp.bfloat16)


def draw_noise_sigma(key, part):
    return sigma_values(key).astype(jnp.float32)


def draw_science(key, part):
    row_kernels, col_kernels = kernel_pair(key)
    destinations, first_rows = piece_routes(key)
    values = piece_values(key)
    sigmas = sigma_values(key)
    mix_key = jax.random.fold_in(key, 51)
    common = 0.5 * jax.random.normal(jax.random.fold_in(mix_key, 1), (1, BASIS), jnp.float32)
    own_part = 0.5 * jax.random.normal(jax.random.fold_in(mix_key, 2), (DEVS, BASIS), jnp.float32)
    mixing = common + own_part
    target = ((destinations * ROWS + first_rows)[:, None] + jnp.arange(BAND, dtype=jnp.int32)[None, :]).reshape(-1)
    coadd_image = jnp.zeros((DEVS * ROWS, COLS), jnp.float32).at[target].add(values.reshape(-1, COLS))
    coadd_image = coadd_image.astype(jnp.bfloat16).astype(jnp.float32)
    mixing_rows = jnp.repeat(mixing, ROWS, axis=0).reshape(CCDS, STRIPS * ROWS, BASIS)

    def one_ccd(inputs):
        picture, weights = inputs
        running = jnp.zeros_like(picture)
        for number in range(BASIS):
            smeared = shifted_sum(shifted_sum(picture, col_kernels[number], 1), row_kernels[number], 0)
            running = running + weights[:, number:number + 1] * smeared
        return running
    clean_image = lax.map(one_ccd, (coadd_image.reshape(CCDS, STRIPS * ROWS, COLS), mixing_rows)).reshape(DEVS * ROWS, COLS)
    noise_key = jax.random.fold_in(key, 52)
    noise_values = jax.random.truncated_normal(noise_key, -5.0, 5.0, (DEVS * ROWS, COLS), jnp.float32)
    return (clean_image + 0.3 * jnp.repeat(sigmas, ROWS)[:, None] * noise_values).astype(jnp.float32)


def draw_band_shift(key, part):
    slot_count = CCDS * RELAY_CAP
    slot_index = jnp.arange(slot_count, dtype=jnp.int32)
    slot_value = slot_index // RELAY_CAP
    first_slot = slot_index % RELAY_CAP == 0
    scores = jax.random.randint(jax.random.fold_in(key, 61), (slot_count,), 0, 2 ** 20, dtype=jnp.int32)
    forced = jax.random.randint(jax.random.fold_in(key, 62), (), 0, CCDS, dtype=jnp.int32)
    reach = ((slot_value == 1) | (slot_value == CCDS // 2)) & first_slot
    scores = jnp.where(reach, -2, scores)
    scores = jnp.where(slot_value == forced, -3, scores)
    scores = scores * slot_count + slot_index
    chosen = jnp.argsort(scores)[:BANDS].astype(jnp.int32)
    shuffle_keys = jax.random.randint(jax.random.fold_in(key, 63), (BANDS,), 0, 2 ** 20, dtype=jnp.int32) * BANDS + jnp.arange(BANDS, dtype=jnp.int32)
    return jnp.take(chosen // RELAY_CAP, jnp.argsort(shuffle_keys)).astype(jnp.int32)


def set_ends(entries, own_key, least, high):
    spot = [jax.random.randint(jax.random.fold_in(own_key, axis), (), 0, length) for axis, length in enumerate(entries.shape)]
    longest = entries.shape.index(max(entries.shape))
    next_to = spot[:longest] + [(spot[longest] + 1) % entries.shape[longest]] + spot[longest + 1:]
    return entries.at[tuple(spot)].set(least).at[tuple(next_to)].set(high)


def scatter_about(own_key, dims, spread, most, held_as=jnp.bfloat16):
    array = jax.random.normal(own_key, dims, jnp.float32) * spread
    return jnp.minimum(jnp.maximum(array, -most), most).astype(held_as)


def setup_inputs(seed: int = 0) -> dict:
    keys = jax.random.split(jax.random.key(seed), 13)
    return {
        "template": draw_template(jax.random.fold_in(keys[12], 71), 0),
        "route_dest": draw_route_dest(jax.random.fold_in(keys[12], 71), 0),
        "route_row": draw_route_row(jax.random.fold_in(keys[12], 71), 0),
        "kern_row": draw_kern_row(jax.random.fold_in(keys[12], 71), 0),
        "kern_col": draw_kern_col(jax.random.fold_in(keys[12], 71), 0),
        "science": draw_science(jax.random.fold_in(keys[12], 71), 0),
        "noise_sigma": draw_noise_sigma(jax.random.fold_in(keys[12], 71), 0),
        "stamp_row": set_ends(jax.random.randint(keys[7], (DEVS * STAMPS,), 0, ROWS - STAMP + 1), jax.random.fold_in(keys[7], 1), 0, ROWS - STAMP).astype(jnp.int32),
        "stamp_col": set_ends(jax.random.randint(keys[8], (DEVS * STAMPS,), 0, COLS - STAMP + 1), jax.random.fold_in(keys[8], 1), 0, COLS - STAMP).astype(jnp.int32),
        "band_shift": draw_band_shift(jax.random.fold_in(keys[12], 71), 0),
        "psf_row": scatter_about(keys[10], (PSF_TAPS,), PSF_TAPS ** -0.5, 1.5),
        "psf_col": scatter_about(keys[11], (PSF_TAPS,), PSF_TAPS ** -0.5, 1.5),
    }


HIGH = lax.Precision.HIGHEST

def lag_table(kernel, block_size):
    tap_count = kernel.shape[1]
    offset = jnp.arange(block_size + tap_count - 1)[:, None] - jnp.arange(block_size)[None, :]
    onehot = (offset[:, :, None] == jnp.arange(tap_count)[None, None, :]).astype(jnp.float32)
    return jnp.einsum('bt,ijt->bij', kernel.astype(jnp.float32), onehot, precision=HIGH)

def column_windows(padded, half_width, block_size):
    height, columns = padded.shape
    block_count = columns // block_size
    wide = jnp.pad(padded, ((0, 0), (half_width, half_width + block_size - 2 * half_width)))
    middle = wide[:, :columns].reshape(height, block_count, block_size)
    border = wide[:, block_size:block_size + columns].reshape(height, block_count, block_size)[:, :, :2 * half_width]
    return jnp.concatenate([middle, border], axis=2)

def row_windows(padded, half_width, block_size):
    height = padded.shape[0] - 2 * half_width
    return jnp.stack([padded[first_row:first_row + block_size + 2 * half_width] for first_row in range(0, height, block_size)], axis=0)

def separable(picture, kernel_rows, kernel_cols, rounding):
    half_width = (kernel_rows.shape[1] - 1) // 2
    height, columns = picture.shape
    padded = jnp.pad(picture.astype(jnp.float32), ((half_width, half_width), (0, 0)))
    windows = column_windows(padded, half_width, min(256, columns))
    col_tables = lag_table(kernel_cols, min(256, columns))
    row_tables = lag_table(kernel_rows, min(256, height))

    def one_kernel(tables):
        col_table, row_table = tables
        across = jnp.einsum('rkc,co->rko', windows, col_table, precision=HIGH).reshape(height + 2 * half_width, columns)
        across = lax.optimization_barrier(across.astype(jnp.bfloat16)).astype(jnp.float32)
        stacked = row_windows(across, half_width, min(256, height))
        return jnp.einsum('ij,kiw->kjw', row_table, stacked, precision=HIGH).reshape(height, columns).astype(rounding)
    return lax.map(one_kernel, (col_tables, row_tables))

def stamp_blocks(picture, corner_rows, corner_cols):

    def single(corner_row, corner_col):
        return lax.dynamic_slice(picture, (jnp.zeros((), jnp.int32), corner_row.astype(jnp.int32), corner_col.astype(jnp.int32)), (picture.shape[0], STAMP, STAMP))
    return jax.vmap(single)(corner_rows, corner_cols)

def reference(template, route_dest, route_row, kern_row, kern_col, science, noise_sigma, stamp_row, stamp_col, band_shift, psf_row, psf_col):
    target = ((route_dest * ROWS + route_row)[:, None] + jnp.arange(BAND, dtype=jnp.int32)[None, :]).reshape(-1)
    coadd_image = jnp.zeros((DEVS * ROWS, COLS), jnp.float32).at[target].add(template.astype(jnp.float32).reshape(-1, COLS))
    coadd_image = coadd_image.astype(jnp.bfloat16).reshape(CCDS, STRIPS * ROWS, COLS)
    sky_image = science.reshape(CCDS, STRIPS * ROWS, COLS)
    weights = (1.0 / (noise_sigma * noise_sigma)).reshape(CCDS, STRIPS)
    corner_rows = (stamp_row.reshape(CCDS, STRIPS, STAMPS) + (jnp.arange(STRIPS, dtype=jnp.int32) * ROWS)[None, :, None]).reshape(CCDS, STRIPS * STAMPS)
    corner_cols = stamp_col.reshape(CCDS, STRIPS * STAMPS)

    def gram_part(inputs):
        picture, sky, weight, tops, lefts = inputs
        basis_images = separable(picture, kern_row, kern_col, jnp.bfloat16)
        basis_cut = stamp_blocks(basis_images, tops, lefts).reshape(STRIPS, STAMPS, BASIS, STAMP * STAMP).astype(jnp.float32)
        sky_cut = stamp_blocks(sky[None], tops, lefts).reshape(STRIPS, STAMPS, STAMP * STAMP)
        gram_matrix = jnp.einsum('skbp,skcp,s->bc', basis_cut, basis_cut, weight, precision=HIGH)
        target_sum = jnp.einsum('skbp,skp,s->b', basis_cut, sky_cut, weight, precision=HIGH)
        return (gram_matrix, target_sum)
    gram_parts, target_parts = lax.map(gram_part, (coadd_image, sky_image, weights, corner_rows, corner_cols))
    gram_matrix = jnp.sum(gram_parts, axis=0)
    target_sum = jnp.sum(target_parts, axis=0)
    factor = jnp.linalg.cholesky(gram_matrix)
    middle = lax.linalg.triangular_solve(factor, target_sum[:, None], left_side=True, lower=True)
    coefficients = lax.linalg.triangular_solve(factor, middle, left_side=True, lower=True, transpose_a=True)[:, 0]
    sigma_rows = jnp.repeat(noise_sigma.reshape(CCDS, STRIPS), ROWS, axis=1)[:, :, None]

    def difference_part(inputs):
        picture, sky, sigma_col = inputs
        basis_images = separable(picture, kern_row, kern_col, jnp.bfloat16)
        model_image = jnp.sum(coefficients[:, None, None] * basis_images.astype(jnp.float32), axis=0)
        return ((sky - model_image) / sigma_col).astype(jnp.bfloat16)
    difference = lax.map(difference_part, (coadd_image, sky_image, sigma_rows)).reshape(DEVS * ROWS, COLS)
    device_rows = stamp_row + jnp.repeat(jnp.arange(DEVS, dtype=jnp.int32) * ROWS, STAMPS)
    stamp_cut = stamp_blocks(difference[None], device_rows, stamp_col).reshape(DEVS * STAMPS, STAMP * STAMP)
    banded = difference.reshape(CCDS, STRIPS, BANDS, BAND, COLS)
    source = (jnp.arange(CCDS, dtype=jnp.int32)[:, None] - band_shift[None, :]) % CCDS
    patch_image = banded[source, :, jnp.arange(BANDS, dtype=jnp.int32)[None, :]]
    patch_image = jnp.transpose(patch_image, (0, 2, 1, 3, 4)).reshape(CCDS, STRIPS * ROWS, COLS)

    def filter_part(picture):
        return separable(picture, psf_row[None, :], psf_col[None, :], jnp.float32)[0]
    filtered = lax.map(filter_part, patch_image).reshape(DEVS * ROWS, COLS)
    return (difference, stamp_cut, coefficients, filtered)
```

```python
import jax
import jax.numpy as jnp
from jax import lax
from jax.experimental import pallas as pl
from jax.experimental.pallas import tpu as pltpu
from jax.sharding import PartitionSpec as P

BASIS = 12
KTAPS = 21
PSF_TAPS = 15
STAMPS = 16
ROWS = 1024
COLS = 512
PAD = 16
FRAMED = ROWS + 2 * PAD
STEP = 224
SPAN = 256
WIN = 56
LANES = BASIS * 32
BOTH = ("ccd", "strip")
SWAP = [(0, 1), (1, 0)]
F32 = jnp.float32
BF16 = jnp.bfloat16
I32 = jnp.int32
HIGH = lax.Precision.HIGHEST

BLOCKS = [(j, min(STEP, ROWS - j), min(SPAN, FRAMED - j)) for j in range(0, ROWS, STEP)]


def vmem():
    return pl.BlockSpec(memory_space=pltpu.VMEM)


def smem():
    return pl.BlockSpec(memory_space=pltpu.SMEM)


def params(mib):
    return pltpu.CompilerParams(vmem_limit_bytes=mib * 2**20)


def iota(shape, dim):
    return lax.broadcasted_iota(I32, shape, dim)


def shape(dims, dtype):
    return jax.ShapeDtypeStruct(dims, dtype)


def cost(flops, moved):
    return pl.CostEstimate(flops=flops, bytes_accessed=moved, transcendentals=0)


def pack_body(dest, row, pieces, out, count, rows):
    devices = out.shape[0]

    def clear(d, c):
        count[d] = 0
        rows[2 * d] = 4096
        rows[2 * d + 1] = 4096
        return c

    lax.fori_loop(0, devices, clear, 0, unroll=8)
    out[...] = jnp.zeros(out.shape, out.dtype)

    def place(i, c):
        d = dest[i]
        k = count[d]
        count[d] = k + 1
        rows[2 * d + k] = row[i]
        piece = pieces[i]
        for q in range(4):
            out[d, 4 * k + q] = piece[:, 128 * q : 128 * (q + 1)]
        return c

    lax.fori_loop(0, pieces.shape[0], place, 0, unroll=8)
    sub, lane = iota((8, 128), 0), iota((8, 128), 1)

    def tell(d, c):
        target = jnp.where(lane < 64, rows[2 * d], rows[2 * d + 1]) + sub
        told = jnp.where((lane & 32) == 0, target >> 5, target & 31)
        out[d, 8] = told.astype(F32).astype(BF16)
        return c

    lax.fori_loop(0, devices, tell, 0, unroll=8)


def pack(route_dest, route_row, template, devices):
    return pl.pallas_call(
        pack_body,
        out_shape=shape((devices, 9, 8, 128), BF16),
        in_specs=[smem(), smem(), vmem()],
        out_specs=vmem(),
        scratch_shapes=[pltpu.SMEM((devices,), I32), pltpu.SMEM((2 * devices,), I32)],
        compiler_params=params(32),
        name="pack",
    )(route_dest, route_row, template)


def band_table(taps, count, size, offset):
    lag = iota((128, 128), 0) - iota((128, 128), 1) + offset
    table = jnp.zeros((128, 128), F32)
    for t in range(count):
        if -127 <= t - offset <= 127:
            table = jnp.where(lag == t, taps(t), table)
    return table.astype(BF16)


def window(ref, first_row, rows, first_col):
    tile = jnp.minimum(jnp.maximum(first_col, 0) >> 7, 2) * 128
    top = jnp.minimum((first_row >> 3) * 8, ref.shape[0] - rows - 8)
    block = ref[pl.ds(pl.multiple_of(top, 8), rows + 8), pl.ds(pl.multiple_of(tile, 128), 256)]
    turn = (256 - (first_col - tile)) & 255
    block = pltpu.roll(block, turn, 1)[:, :128]
    return pltpu.roll(block, lax.rem(rows + 8 - (first_row - top), rows + 8), 0)[:rows]


def tables_body(
    kr, kc, pr, pc, kcl, shift, srow, scol, science,
    cols_out, rows_out, pcols_out, prows_out, stamp_out, slot_out, pick_out, sky_out, count,
):
    for b in range(BASIS):
        for k in range(3):
            cols_out[b, k] = band_table(lambda t: kc[b, t], KTAPS, 128, 10 + 128 * (k - 1))
        for k in range(2):
            lag = iota((128, 128), 1) - iota((128, 128), 0) - 6 + 128 * k
            table = jnp.zeros((128, 128), F32)
            for t in range(KTAPS):
                table = jnp.where(lag == t, kr[b, t], table)
            rows_out[b, k] = table.astype(BF16)
    for k in range(3):
        pcols_out[k] = band_table(lambda t: pc[t], PSF_TAPS, 128, 7 + 128 * (k - 1))
    for k in range(2):
        lag = iota((128, 128), 1) - iota((128, 128), 0) - 9 + 128 * k
        table = jnp.zeros((128, 128), F32)
        for t in range(PSF_TAPS):
            table = jnp.where(lag == t, pr[t], table)
        prows_out[k] = table.astype(BF16)
    lag = iota((128, LANES), 0) - (iota((128, LANES), 1) & 31)
    table = jnp.zeros((128, LANES), F32)
    for t in range(KTAPS):
        table = jnp.where(lag == t, kcl[t : t + 1, :], table)
    stamp_out[...] = table.astype(BF16)

    own, ccds = lax.axis_index("ccd"), lax.axis_size("ccd")
    cap = slot_out.shape[0] * 2 // ccds

    def clear(v, c):
        count[v] = 0
        return c

    lax.fori_loop(0, ccds, clear, 0)

    def seat(m, c):
        v = shift[m]
        k = count[v]
        count[v] = k + 1
        slot_out[m] = lax.rem(own + v, ccds) * cap + k
        pick_out[m] = lax.rem(own - v + ccds, ccds) * cap + k
        return c

    lax.fori_loop(0, slot_out.shape[0], seat, 0)
    lane = iota((32, 128), 1)

    def cut(s, c):
        sky = jnp.where(lane < 32, window(science, srow[s], 32, scol[s]), 0.0)
        sky = sky + pltpu.roll(sky, 32, 1)
        sky_out[s] = sky + pltpu.roll(sky, 64, 1)
        return c

    lax.fori_loop(0, STAMPS, cut, 0)


def tables(kern_row, kern_col, psf_row, psf_col, band_shift, stamp_row, stamp_col, science):
    kc = kern_col.astype(F32)
    lanes = jnp.pad(jnp.repeat(kc.T, 32, axis=1), ((0, 3), (0, 0)))
    return pl.pallas_call(
        tables_body,
        out_shape=(
            shape((BASIS, 3, 128, 128), BF16),
            shape((BASIS, 2, 128, 128), BF16),
            shape((3, 128, 128), BF16),
            shape((2, 128, 128), BF16),
            shape((128, LANES), BF16),
            shape(band_shift.shape, I32),
            shape(band_shift.shape, I32),
            shape((STAMPS, 32, 128), F32),
        ),
        in_specs=[smem()] * 4 + [vmem()] + [smem()] * 3 + [vmem()],
        out_specs=(vmem(),) * 5 + (smem(),) * 2 + (vmem(),),
        scratch_shapes=[pltpu.SMEM((64,), I32)],
        compiler_params=params(32),
        cost_estimate=cost(2 * 10**9, 4 * 10**6),
        name="tables",
    )(
        kern_row.astype(F32), kc, psf_row.astype(F32), psf_col.astype(F32), lanes,
        band_shift, stamp_row, stamp_col, science,
    )


def coadd_body(arrived, out, edge, held):
    senders = arrived.shape[0]
    half = senders * 8
    told = arrived[:, 8].astype(F32).reshape(half, 128).T
    target = jnp.concatenate(
        [told[64 * k : 64 * k + 1] * 32.0 + told[64 * k + 32 : 64 * k + 33] for k in range(2)], axis=1
    ).astype(I32)
    for k in range(2):
        for q in range(4):
            part = arrived[:, 4 * k + q].astype(F32).reshape(half, 128)
            held[half * k : half * (k + 1), 128 * q : 128 * (q + 1)] = part.astype(BF16)
    for m in range(0, ROWS, 256):
        hit = (iota((256, 2 * half), 0) + m) == target
        placer = jnp.where(hit, 1.0, 0.0).astype(BF16)
        out[m : m + 256] = jnp.dot(placer, held[...], preferred_element_type=F32).astype(BF16)
    strip = lax.axis_index("strip")

    @pl.when(strip == 0)
    def _():
        edge[...] = out[ROWS - PAD :]

    @pl.when(strip != 0)
    def _():
        edge[...] = out[:PAD]


def coadd(arrived):
    senders = arrived.shape[0]
    return pl.pallas_call(
        coadd_body,
        out_shape=(shape((ROWS, COLS), BF16), shape((PAD, COLS), BF16)),
        in_specs=[vmem()],
        out_specs=(vmem(), vmem()),
        scratch_shapes=[pltpu.VMEM((senders * 16, COLS), BF16)],
        compiler_params=params(40),
        name="coadd",
    )(arrived)


def frame(framed, image, near):
    strip = lax.axis_index("strip")
    rows = near[...].astype(F32)
    framed[PAD : PAD + ROWS] = image[...].astype(framed.dtype)
    framed[:PAD] = jnp.where(strip == 0, 0.0, rows).astype(framed.dtype)
    framed[PAD + ROWS :] = jnp.where(strip == 0, rows, 0.0).astype(framed.dtype)


def stamps_body(image, near, sigma, srow, scol, table, krl, sky, out, framed, wins, across, basis):
    frame(framed, image, near)
    lane = iota((WIN, 128), 1)

    def cut(s, c):
        first = scol[s] - 10
        block = window(framed, srow[s] + 6, WIN, first)
        inside = (lane < 52) & (lane + first >= 0) & (lane + first < COLS)
        wins[s] = jnp.where(inside, block, 0.0)
        return c

    lax.fori_loop(0, STAMPS, cut, 0, unroll=2)
    wide = jnp.dot(
        wins[...].reshape(STAMPS * WIN, 128).astype(BF16), table[...], preferred_element_type=F32
    )
    across[...] = wide.astype(BF16).astype(F32).reshape(STAMPS, WIN, LANES)

    def rows(s, total):
        parts = []
        for q in range(3):
            acc = jnp.zeros((32, 128), F32)
            for t in range(KTAPS):
                acc = acc + krl[t : t + 1, 128 * q : 128 * q + 128] * across[s, t : t + 32, 128 * q : 128 * q + 128]
            done = acc.astype(BF16)
            basis[pl.ds(pl.multiple_of(s * 32, 32), 32), 128 * q : 128 * q + 128] = done
            parts.append(total[q] + jnp.sum(done.astype(F32) * sky[s], axis=0, keepdims=True))
        return tuple(parts)

    total = lax.fori_loop(0, STAMPS, rows, tuple(jnp.zeros((1, 128), F32) for _ in range(3)))
    total = jnp.concatenate(total, axis=1)
    pairs = lax.dot_general(
        basis[...], basis[...], (((0,), (0,)), ((), ())), preferred_element_type=F32
    )
    same = (iota((LANES, LANES), 0) & 31) == (iota((LANES, LANES), 1) & 31)
    pairs = jnp.where(same, pairs, 0.0)
    left = ((iota((16, LANES), 1) >> 5) == iota((16, LANES), 0)).astype(F32)
    right = ((iota((LANES, 128), 0) >> 5) == (iota((LANES, 128), 1) & 15)).astype(F32)
    gram = jnp.dot(jnp.dot(left, pairs, precision=HIGH, preferred_element_type=F32), right,
                   precision=HIGH, preferred_element_type=F32)
    goal = jnp.sum(left * total, axis=1, keepdims=True)
    row, col = iota((16, 128), 0), iota((16, 128), 1)
    both = jnp.where((col & 15) == BASIS, goal, gram)
    both = jnp.where((col >> 4) == (row & 7), both, 0.0) / (sigma[0] * sigma[0])
    packed = jnp.concatenate(
        [jnp.sum(both[:8], axis=0, keepdims=True), jnp.sum(both[8:], axis=0, keepdims=True)], axis=0
    )
    out[...] = jnp.broadcast_to(packed[None], out.shape)


def stamp_sums(image, near, sigma, srow, scol, table, krl, sky, devices):
    return pl.pallas_call(
        stamps_body,
        out_shape=shape((devices, 2, 128), F32),
        in_specs=[vmem(), vmem(), smem(), smem(), smem(), vmem(), vmem(), vmem()],
        out_specs=vmem(),
        scratch_shapes=[
            pltpu.VMEM((FRAMED, COLS), F32),
            pltpu.VMEM((STAMPS, WIN, 128), F32),
            pltpu.VMEM((STAMPS, WIN, LANES), F32),
            pltpu.VMEM((STAMPS * 32, LANES), BF16),
        ],
        compiler_params=params(40),
        name="stamp_sums",
    )(image, near, sigma, srow, scol, table, krl, sky)


def fill_cols(wide, blocks):
    for i in range(4):
        for o in range(4):
            if abs(i - o) <= 1:
                wide[128 * i : 128 * i + 128, 128 * o : 128 * o + 128] = blocks[i - o + 1]
            else:
                wide[128 * i : 128 * i + 128, 128 * o : 128 * o + 128] = jnp.zeros((128, 128), BF16)


def across_body(image, near, blocks, out, framed, wide):
    @pl.when(pl.program_id(0) == 0)
    def _():
        frame(framed, image, near)

    fill_cols(wide, blocks[0])
    for m in range(0, FRAMED, 352):
        out[0, m : m + 352] = jnp.dot(
            framed[m : m + 352], wide[...], preferred_element_type=F32
        ).astype(BF16)


def across_all(image, near, blocks):
    return pl.pallas_call(
        across_body,
        grid=(BASIS,),
        out_shape=shape((BASIS, FRAMED, COLS), BF16),
        in_specs=[
            pl.BlockSpec((ROWS, COLS), lambda b: (0, 0)),
            pl.BlockSpec((PAD, COLS), lambda b: (0, 0)),
            pl.BlockSpec((1, 3, 128, 128), lambda b: (b, 0, 0, 0)),
        ],
        out_specs=pl.BlockSpec((1, FRAMED, COLS), lambda b: (b, 0, 0)),
        scratch_shapes=[pltpu.VMEM((FRAMED, COLS), BF16), pltpu.VMEM((COLS, COLS), BF16)],
        compiler_params=params(32),
        cost_estimate=cost(2 * BASIS * FRAMED * COLS * COLS, 16 * 10**6),
        name="across",
    )(image, near, blocks)


def solve(sums):
    total = jnp.sum(sums[...], axis=0)
    row, col = iota((16, 128), 0), iota((16, 128), 1)
    both = jnp.where(row < 8, total[0:1], total[1:2])
    both = jnp.where((col >> 4) == (row & 7), both, 0.0)
    for turn in (64, 32, 16):
        both = both + pltpu.roll(both, turn, 1)
    for k in range(BASIS):
        pivot = both[k : k + 1] / both[k : k + 1, k : k + 1]
        both = jnp.where(row == k, pivot, both - both[:, k : k + 1] * pivot)
    return both[:, BASIS : BASIS + 1]


def fill_rows(table, blocks):
    table[:128, :128] = blocks[0]
    table[:128, 128:] = blocks[1]
    table[128:, :128] = jnp.zeros((STEP - 128, 128), BF16)
    table[128:, 128:] = blocks[0][: STEP - 128]


def difference_body(
    sums, across, blocks, science, sigma, slot, coef_out, diff_out, leave_out, model, coef, table
):
    b = pl.program_id(0)

    @pl.when(b == 0)
    def _():
        found = solve(sums)
        coef[...] = jnp.broadcast_to(found, coef.shape)
        eye = iota((16, 128), 0) == iota((16, 128), 1)
        coef_out[...] = jnp.sum(jnp.where(eye, found, 0.0), axis=0, keepdims=True)
        model[...] = jnp.zeros(model.shape, F32)

    fill_rows(table, blocks[0])
    weight = coef[pl.ds(b, 1), :]
    for first, rows, span in BLOCKS:
        basis = jnp.dot(
            table[:rows, :span], across[0, first : first + span], preferred_element_type=F32
        )
        model[first : first + rows] += weight * basis.astype(BF16).astype(F32)

    @pl.when(b == BASIS - 1)
    def _():
        scale = 1.0 / sigma[0]

        def finish(m, c):
            rows = pl.ds(pl.multiple_of(m * 16, 16), 16)
            left = (science[rows] - model[rows]) * scale
            diff_out[rows] = left.astype(BF16)
            leave_out[slot[2 * m]] = left[:8].astype(BF16)
            leave_out[slot[2 * m + 1]] = left[8:].astype(BF16)
            return c

        lax.fori_loop(0, ROWS // 16, finish, 0, unroll=4)


def difference_all(sums, across, blocks, science, sigma, slot, slots):
    whole = lambda *dims: pl.BlockSpec(dims, lambda b: (0,) * len(dims))
    return pl.pallas_call(
        difference_body,
        grid=(BASIS,),
        out_shape=(shape((1, 128), F32), shape((ROWS, COLS), BF16), shape((slots, 8, COLS), BF16)),
        in_specs=[
            whole(*sums.shape),
            pl.BlockSpec((1, FRAMED, COLS), lambda b: (b, 0, 0)),
            pl.BlockSpec((1, 2, 128, 128), lambda b: (b, 0, 0, 0)),
            whole(ROWS, COLS),
            smem(),
            smem(),
        ],
        out_specs=(whole(1, 128), whole(ROWS, COLS), whole(slots, 8, COLS)),
        scratch_shapes=[
            pltpu.VMEM((ROWS, COLS), F32),
            pltpu.VMEM((16, COLS), F32),
            pltpu.VMEM((STEP, SPAN), BF16),
        ],
        compiler_params=params(40),
        name="difference",
    )(sums, across, blocks, science, sigma, slot)


def cut_body(diff, srow, scol, out, wide):
    wide[...] = diff[...].astype(F32)
    row, lane = iota((32, 128), 0), iota((32, 128), 1)
    pick = (iota((8, 32), 1) >> 2 == iota((8, 32), 0)).astype(BF16)

    def cut(s, c):
        block = jnp.where(lane < 32, window(wide, srow[s], 32, scol[s]), 0.0)
        block = block + pltpu.roll(block, 32, 1)
        block = block + pltpu.roll(block, 64, 1)
        block = jnp.where((lane >> 5) == (row & 3), block, 0.0).astype(BF16)
        out[s] = jnp.dot(pick, block, preferred_element_type=F32).astype(BF16)
        return c

    lax.fori_loop(0, STAMPS, cut, 0)


def cut_stamps(diff, srow, scol):
    return pl.pallas_call(
        cut_body,
        out_shape=shape((STAMPS, 8, 128), BF16),
        in_specs=[vmem(), smem(), smem()],
        out_specs=vmem(),
        scratch_shapes=[pltpu.VMEM((ROWS, COLS), F32)],
        compiler_params=params(32),
        cost_estimate=cost(10**8, 3 * 10**6),
        name="cut_stamps",
    )(diff, srow, scol)


def smooth_body(landed, pick, blocks, out, patch, wide):
    fill_cols(wide, blocks)
    for first in range(0, ROWS, 256):

        def gather(m, c):
            pair = jnp.concatenate(
                [landed[pick[2 * m]].astype(F32), landed[pick[2 * m + 1]].astype(F32)], axis=0
            )
            patch[pl.ds(pl.multiple_of(m * 16, 16), 16)] = pair.astype(BF16)
            return c

        lax.fori_loop(first // 16, first // 16 + 16, gather, 0, unroll=4)
        out[first : first + 256] = jnp.dot(
            patch[first : first + 256], wide[...], preferred_element_type=F32
        ).astype(BF16)


def smooth(landed, pick, blocks):
    return pl.pallas_call(
        smooth_body,
        out_shape=shape((ROWS, COLS), BF16),
        in_specs=[vmem(), smem(), vmem()],
        out_specs=vmem(),
        scratch_shapes=[pltpu.VMEM((ROWS, COLS), BF16), pltpu.VMEM((COLS, COLS), BF16)],
        compiler_params=params(32),
        cost_estimate=cost(2 * ROWS * COLS * COLS, 3 * 10**6),
        name="smooth",
    )(landed, pick, blocks)


def filter_body(smoothed, near, cblocks, rblocks, out, framed, wide, table, tail):
    fill_cols(wide, cblocks)
    fill_rows(table, rblocks)
    tail[...] = jnp.concatenate(
        [near[...].astype(F32), jnp.zeros((8, COLS), F32)], axis=0
    ).astype(BF16)
    edge = jnp.dot(tail[...], wide[...], preferred_element_type=F32)
    edge = jnp.where(lax.axis_index("strip") == 0, edge, jnp.concatenate([edge[8:], edge[:8]], axis=0))
    frame(framed, smoothed, edge.astype(BF16))
    for first, rows, span in BLOCKS:
        out[first : first + rows] = jnp.dot(
            table[:rows, :span], framed[first : first + span], preferred_element_type=F32
        )


def filter_rows(smoothed, near, cblocks, rblocks):
    return pl.pallas_call(
        filter_body,
        out_shape=shape((ROWS, COLS), F32),
        in_specs=[vmem()] * 4,
        out_specs=vmem(),
        scratch_shapes=[
            pltpu.VMEM((FRAMED, COLS), BF16),
            pltpu.VMEM((COLS, COLS), BF16),
            pltpu.VMEM((STEP, SPAN), BF16),
            pltpu.VMEM((PAD, COLS), BF16),
        ],
        compiler_params=params(32),
        name="filter_rows",
    )(smoothed, near, cblocks, rblocks)


def shards(
    template, route_dest, route_row, kern_row, kern_col, science, noise_sigma,
    stamp_row, stamp_col, band_shift, psf_row, psf_col,
):
    ccds = lax.axis_size("ccd")
    devices = ccds * lax.axis_size("strip")
    bands = band_shift.shape[0]
    cap = 2 * bands // ccds
    outgoing = pack(route_dest, route_row, template, devices)
    arrived = lax.all_to_all(outgoing, BOTH, split_axis=0, concat_axis=0, tiled=True)
    cols, rows, pcols, prows, stamp_table, slot, pick, sky = tables(
        kern_row, kern_col, psf_row, psf_col, band_shift, stamp_row, stamp_col, science
    )
    krl = jnp.pad(jnp.repeat(kern_row.astype(F32).T, 32, axis=1), ((0, 3), (0, 0)))
    image, edge = coadd(arrived)
    near = lax.ppermute(edge, "strip", SWAP)
    sums = stamp_sums(
        image, near, noise_sigma, stamp_row, stamp_col, stamp_table, krl, sky, devices
    )
    sums = lax.all_to_all(sums, BOTH, split_axis=0, concat_axis=0, tiled=True)
    across = across_all(image, near, cols)
    coef, diff, leaving = difference_all(
        sums, across, rows, science, noise_sigma, slot, ccds * cap
    )
    landed = lax.all_to_all(
        leaving.reshape(ccds, cap, 8, COLS), "ccd", split_axis=0, concat_axis=0, tiled=True
    ).reshape(ccds * cap, 8, COLS)
    stamp_cut = cut_stamps(diff, stamp_row, stamp_col).reshape(STAMPS, 1024)
    last = jnp.where(lax.axis_index("strip") == 0, pick[bands - 1], pick[0])
    beside = lax.ppermute(
        lax.dynamic_slice(landed, (last, 0, 0), (1, 8, COLS))[0], "strip", SWAP
    )
    smoothed = smooth(landed, pick, pcols)
    filtered = filter_rows(smoothed, beside, pcols, prows)
    return (diff, stamp_cut, coef[0, :BASIS], filtered)


def solution(mesh):
    placed = (
        P(BOTH, None, None), P(BOTH), P(BOTH), P(), P(), P(BOTH, None),
        P(BOTH), P(BOTH), P(BOTH), P(), P(), P(),
    )
    return jax.shard_map(
        shards,
        mesh=mesh,
        in_specs=placed,
        out_specs=(P(BOTH, None), P(BOTH, None), P(), P(BOTH, None)),
        check_vma=False,
    )
```

```python
import jax
import jax.numpy as jnp
from jax import lax
from jax.experimental import pallas as pl
from jax.experimental.pallas import tpu as pltpu
from jax.sharding import PartitionSpec as P

BASIS = 12
KTAPS = 21
PSF_TAPS = 15
STAMPS = 16
ROWS = 1024
COLS = 512
PAD = 16
FRAMED = ROWS + 2 * PAD
STEP = 224
SPAN = 256
WIN = 56
LANES = BASIS * 32
LARGE = 58
BOTH = ("ccd", "strip")
SWAP = [(0, 1), (1, 0)]
F32 = jnp.float32
BF16 = jnp.bfloat16
I32 = jnp.int32
HIGH = lax.Precision.HIGHEST

BLOCKS = [(j, min(STEP, ROWS - j), min(SPAN, FRAMED - j)) for j in range(0, ROWS, STEP)]


def vmem():
    return pl.BlockSpec(memory_space=pltpu.VMEM)


def hbm():
    return pl.BlockSpec(memory_space=pltpu.HBM)


def smem():
    return pl.BlockSpec(memory_space=pltpu.SMEM)


def params(mib):
    return pltpu.CompilerParams(vmem_limit_bytes=mib * 2**20)


def iota(shape, dim):
    return lax.broadcasted_iota(I32, shape, dim)


def shape(dims, dtype):
    return jax.ShapeDtypeStruct(dims, dtype)


def cost(flops, moved):
    return pl.CostEstimate(flops=flops, bytes_accessed=moved, transcendentals=0)


CHUNKS = 8


def pack_body(dest_in, row_in, pieces_in, sent, dest, row, pieces, out, count, rows, sems):
    devices = out.shape[0]
    loads = [
        pltpu.make_async_copy(src, dst, sems.at[CHUNKS + i])
        for i, (src, dst) in enumerate([(dest_in, dest), (row_in, row), (pieces_in, pieces)])
    ]
    for load in loads:
        load.start()
    out[...] = jnp.zeros(out.shape, out.dtype)

    def clear(d, c):
        count[d] = 0
        rows[2 * d] = 4096
        rows[2 * d + 1] = 4096
        return c

    lax.fori_loop(0, devices, clear, 0, unroll=8)
    for load in loads:
        load.wait()

    def place(i, c):
        d = dest[i]
        k = count[d]
        count[d] = k + 1
        rows[2 * d + k] = row[i]
        piece = pieces[i]
        for q in range(4):
            out[d, 4 * k + q] = piece[:, 128 * q : 128 * (q + 1)]
        return c

    lax.fori_loop(0, pieces.shape[0], place, 0, unroll=8)
    sub, lane = iota((8, 128), 0), iota((8, 128), 1)

    def tell(d, c):
        target = jnp.where(lane < 64, rows[2 * d], rows[2 * d + 1]) + sub
        told = jnp.where((lane & 32) == 0, target >> 5, target & 31)
        out[d, 8] = told.astype(F32).astype(BF16)
        return c

    part = devices // CHUNKS
    sends = []
    for i in range(CHUNKS):
        lax.fori_loop(i * part, (i + 1) * part, tell, 0, unroll=8)
        some = pl.ds(i * part, part)
        sends.append(pltpu.make_async_copy(out.at[some], sent.at[some], sems.at[i]))
        sends[-1].start()
    for send in sends:
        send.wait()


def pack(route_dest, route_row, template, devices):
    pieces = template.shape[0]
    return pl.pallas_call(
        pack_body,
        out_shape=shape((devices, 9, 8, 128), BF16),
        in_specs=[hbm()] * 3,
        out_specs=hbm(),
        scratch_shapes=[
            pltpu.SMEM((pieces,), I32),
            pltpu.SMEM((pieces,), I32),
            pltpu.VMEM(template.shape, BF16),
            pltpu.VMEM((devices, 9, 8, 128), BF16),
            pltpu.SMEM((devices,), I32),
            pltpu.SMEM((2 * devices,), I32),
            pltpu.SemaphoreType.DMA((CHUNKS + 3,)),
        ],
        compiler_params=params(LARGE),
        name="pack",
    )(route_dest, route_row, template)


def band_table(taps, count, size, offset):
    lag = iota((128, 128), 0) - iota((128, 128), 1) + offset
    table = jnp.zeros((128, 128), F32)
    for t in range(count):
        if -127 <= t - offset <= 127:
            table = jnp.where(lag == t, taps(t), table)
    return table.astype(BF16)


def window(ref, first_row, rows, first_col):
    tile = jnp.minimum(jnp.maximum(first_col, 0) >> 7, 2) * 128
    top = jnp.minimum((first_row >> 3) * 8, ref.shape[0] - rows - 8)
    block = ref[pl.ds(pl.multiple_of(top, 8), rows + 8), pl.ds(pl.multiple_of(tile, 128), 256)]
    turn = (256 - (first_col - tile)) & 255
    block = pltpu.roll(block, turn, 1)[:, :128]
    return pltpu.roll(block, lax.rem(rows + 8 - (first_row - top), rows + 8), 0)[:rows]


def tables_body(
    kr, kc, pr, pc, kcl, krl, shift, srow, scol, science,
    cols_out, rows_out, pcols_out, prows_out, stamp_out, krl_out, seam_out,
    slot_out, pick_out, sky_out, count,
):
    for b in range(BASIS):
        for k in range(3):
            cols_out[b, k] = band_table(lambda t: kc[b, t], KTAPS, 128, 10 + 128 * (k - 1))
        for k in range(2):
            lag = iota((128, 128), 1) - iota((128, 128), 0) - 6 + 128 * k
            table = jnp.zeros((128, 128), F32)
            for t in range(KTAPS):
                table = jnp.where(lag == t, kr[b, t], table)
            table = table.astype(BF16)
            rows_out[b, :128, 128 * k : 128 * k + 128] = table
            if k == 0:
                rows_out[b, 128:, 128:] = table[: STEP - 128]
                rows_out[b, 128:, :128] = jnp.zeros((STEP - 128, 128), BF16)
    for k in range(3):
        pcols_out[k] = band_table(lambda t: pc[t], PSF_TAPS, 128, 7 + 128 * (k - 1))
    for k in range(2):
        lag = iota((128, 128), 1) - iota((128, 128), 0) - 9 + 128 * k
        table = jnp.zeros((128, 128), F32)
        for t in range(PSF_TAPS):
            table = jnp.where(lag == t, pr[t], table)
        prows_out[k] = table.astype(BF16)
    lag = iota((128, LANES), 0) - (iota((128, LANES), 1) & 31)
    table = jnp.zeros((128, LANES), F32)
    for t in range(KTAPS):
        table = jnp.where(lag == t, kcl[t : t + 1, :], table)
    stamp_out[...] = table.astype(BF16)
    krl_out[...] = krl[...]
    seam_out[...] = jnp.zeros(seam_out.shape, BF16)
    place = ((iota((32, 128), 1) + 16) & 31) - 16
    source = iota((32, 128), 0) - 16
    crosses = (place >= -10) & (place < 10) & ((place < 0) != (source < 0))
    lag = jnp.where(crosses, source - place + 10, -1)
    for v in range(3):
        taps = pltpu.roll(kcl[:, 128 * v : 128 * v + 128], 112, 1)
        table = jnp.zeros((32, 128), F32)
        for t in range(KTAPS):
            table = jnp.where(lag == t, taps[t : t + 1, :], table)
        seam_out[112:144, 128 * v : 128 * v + 128] = table.astype(BF16)

    own, ccds = lax.axis_index("ccd"), lax.axis_size("ccd")
    cap = slot_out.shape[0] * 2 // ccds

    def clear(v, c):
        count[v] = 0
        return c

    lax.fori_loop(0, ccds, clear, 0)

    def seat(m, c):
        v = shift[m]
        k = count[v]
        count[v] = k + 1
        slot_out[m] = lax.rem(own + v, ccds) * cap + k
        pick_out[m] = lax.rem(own - v + ccds, ccds) * cap + k
        return c

    lax.fori_loop(0, slot_out.shape[0], seat, 0)
    lane = iota((32, 128), 1)

    def cut(s, c):
        sky = jnp.where(lane < 32, window(science, srow[s], 32, scol[s]), 0.0)
        sky = sky + pltpu.roll(sky, 32, 1)
        sky_out[s] = sky + pltpu.roll(sky, 64, 1)
        return c

    lax.fori_loop(0, STAMPS, cut, 0)


def tables(kern_row, kern_col, psf_row, psf_col, band_shift, stamp_row, stamp_col, science):
    kc = kern_col.astype(F32)
    expand = lambda taps: jnp.pad(jnp.repeat(taps.T, 32, axis=1), ((0, 3), (0, 0)))
    return pl.pallas_call(
        tables_body,
        out_shape=(
            shape((BASIS, 3, 128, 128), BF16),
            shape((BASIS, STEP, SPAN), BF16),
            shape((3, 128, 128), BF16),
            shape((2, 128, 128), BF16),
            shape((128, LANES), BF16),
            shape((24, LANES), F32),
            shape((256, LANES), BF16),
            shape(band_shift.shape, I32),
            shape(band_shift.shape, I32),
            shape((STAMPS, 32, 128), F32),
        ),
        in_specs=[smem()] * 4 + [vmem()] * 2 + [smem()] * 3 + [vmem()],
        out_specs=(vmem(),) * 7 + (smem(),) * 2 + (vmem(),),
        scratch_shapes=[pltpu.SMEM((64,), I32)],
        compiler_params=params(16),
        cost_estimate=cost(2 * 10**9, 4 * 10**6),
        name="tables",
    )(
        kern_row.astype(F32), kc, psf_row.astype(F32), psf_col.astype(F32),
        expand(kc), expand(kern_row.astype(F32)),
        band_shift, stamp_row, stamp_col, science,
    )


def coadd_body(arrived, ready, out, edge, held):
    senders = arrived.shape[0]
    half = senders * 8
    told = arrived[:, 8].astype(F32).reshape(half, 128).T
    target = jnp.concatenate(
        [told[64 * k : 64 * k + 1] * 32.0 + told[64 * k + 32 : 64 * k + 33] for k in range(2)], axis=1
    ).astype(I32)
    for k in range(2):
        for q in range(4):
            part = arrived[:, 4 * k + q].astype(F32).reshape(half, 128)
            held[half * k : half * (k + 1), 128 * q : 128 * (q + 1)] = part.astype(BF16)
    for m in range(0, ROWS, 256):
        hit = (iota((256, 2 * half), 0) + m) == target
        placer = jnp.where(hit, 1.0, 0.0).astype(BF16)
        out[m : m + 256] = jnp.dot(placer, held[...], preferred_element_type=F32).astype(BF16)
    strip = lax.axis_index("strip")

    @pl.when(strip == 0)
    def _():
        edge[...] = out[ROWS - PAD :]

    @pl.when(strip != 0)
    def _():
        edge[...] = out[:PAD]


def coadd(arrived, ready):
    senders = arrived.shape[0]
    return pl.pallas_call(
        coadd_body,
        out_shape=(shape((ROWS, COLS), BF16), shape((PAD, COLS), BF16)),
        in_specs=[vmem(), pl.BlockSpec(memory_space=pl.ANY)],
        out_specs=(vmem(), vmem()),
        scratch_shapes=[pltpu.VMEM((senders * 16, COLS), BF16)],
        compiler_params=params(16),
        name="coadd",
    )(arrived, ready)


def frame(framed, image, near):
    strip = lax.axis_index("strip")
    rows = near[...].astype(F32)
    framed[PAD : PAD + ROWS] = image[...].astype(framed.dtype)
    framed[:PAD] = jnp.where(strip == 0, 0.0, rows).astype(framed.dtype)
    framed[PAD + ROWS :] = jnp.where(strip == 0, rows, 0.0).astype(framed.dtype)


def stamps_body(image, near, sigma, srow, scol, table, krl, sky, out, framed, wins, across, basis):
    frame(framed, image, near)
    lane = iota((WIN, 128), 1)

    def cut(s, c):
        first = scol[s] - 10
        block = window(framed, srow[s] + 6, WIN, first)
        inside = (lane < 52) & (lane + first >= 0) & (lane + first < COLS)
        wins[s] = jnp.where(inside, block, 0.0)
        return c

    lax.fori_loop(0, STAMPS, cut, 0, unroll=2)
    wide = jnp.dot(
        wins[...].reshape(STAMPS * WIN, 128).astype(BF16), table[...], preferred_element_type=F32
    )
    across[...] = wide.astype(BF16).astype(F32).reshape(STAMPS, WIN, LANES)

    def rows(s, total):
        parts = []
        for q in range(3):
            acc = jnp.zeros((32, 128), F32)
            for t in range(KTAPS):
                acc = acc + krl[t : t + 1, 128 * q : 128 * q + 128] * across[s, t : t + 32, 128 * q : 128 * q + 128]
            done = acc.astype(BF16)
            basis[pl.ds(pl.multiple_of(s * 32, 32), 32), 128 * q : 128 * q + 128] = done
            parts.append(total[q] + jnp.sum(done.astype(F32) * sky[s], axis=0, keepdims=True))
        return tuple(parts)

    total = lax.fori_loop(0, STAMPS, rows, tuple(jnp.zeros((1, 128), F32) for _ in range(3)))
    total = jnp.concatenate(total, axis=1)
    pairs = lax.dot_general(
        basis[...], basis[...], (((0,), (0,)), ((), ())), preferred_element_type=F32
    )
    same = (iota((LANES, LANES), 0) & 31) == (iota((LANES, LANES), 1) & 31)
    pairs = jnp.where(same, pairs, 0.0)
    gram = [jnp.sum(pairs[32 * b : 32 * b + 32], axis=0, keepdims=True) for b in range(BASIS)]
    gram = jnp.concatenate(gram + [total, jnp.zeros((3, LANES), F32)], axis=0)
    parts = []
    for q in range(3):
        part = gram[:, 128 * q : 128 * q + 128]
        for turn in (1, 2, 4, 8, 16):
            part = part + pltpu.roll(part, 128 - turn, 1)
        parts.append(part)
    row, col = iota((16, 128), 0), iota((16, 128), 1)
    both = jnp.zeros((16, 128), F32)
    goal = jnp.zeros((16, 1), F32)
    for b in range(BASIS):
        entry = parts[b // 4][:, 32 * (b & 3) : 32 * (b & 3) + 1]
        both = jnp.where((col & 15) == b, entry, both)
        goal = jnp.where(row[:, :1] == b, entry[BASIS : BASIS + 1], goal)
    both = jnp.where((col & 15) == BASIS, goal, both)
    both = jnp.where(((col >> 4) == (row & 7)) & (row < BASIS), both, 0.0)
    both = both / (sigma[0] * sigma[0])
    packed = jnp.concatenate(
        [jnp.sum(both[:8], axis=0, keepdims=True), jnp.sum(both[8:], axis=0, keepdims=True)], axis=0
    )
    out[...] = jnp.broadcast_to(packed[None], out.shape)


def stamp_sums(image, near, sigma, srow, scol, table, krl, sky, devices):
    return pl.pallas_call(
        stamps_body,
        out_shape=shape((devices, 2, 128), F32),
        in_specs=[vmem(), vmem(), smem(), smem(), smem(), vmem(), vmem(), vmem()],
        out_specs=vmem(),
        scratch_shapes=[
            pltpu.VMEM((FRAMED, COLS), F32),
            pltpu.VMEM((STAMPS, WIN, 128), F32),
            pltpu.VMEM((STAMPS, WIN, LANES), F32),
            pltpu.VMEM((STAMPS * 32, LANES), BF16),
        ],
        compiler_params=params(16),
        name="stamp_sums",
    )(image, near, sigma, srow, scol, table, krl, sky)


def fill_cols(wide, blocks):
    for i in range(4):
        for o in range(4):
            if abs(i - o) <= 1:
                wide[128 * i : 128 * i + 128, 128 * o : 128 * o + 128] = blocks[i - o + 1]
            else:
                wide[128 * i : 128 * i + 128, 128 * o : 128 * o + 128] = jnp.zeros((128, 128), BF16)


def across_body(image, near, blocks, seam, out, framed, wide, border, held, sems):
    frame(framed, image, near)
    for m in range(0, FRAMED, 352):
        for v in range(3):
            border[v, m : m + 352] = jnp.dot(
                framed[m : m + 352, 128:384],
                seam[:, 128 * v : 128 * v + 128],
                preferred_element_type=F32,
            )
    lane = iota((352, 128), 1)

    def save(b, g):
        return pltpu.make_async_copy(held.at[g], out.at[b], sems.at[g])

    def four(v, c):
        for g in range(4):
            b = 4 * v + g
            for i in range(2):
                for o in range(2):
                    wide[128 * i : 128 * i + 128, 128 * o : 128 * o + 128] = blocks[b, i - o + 1]

            @pl.when(v > 0)
            def _():
                save(b - 4, g).wait()

            for m in range(0, FRAMED, 352):
                rows = slice(m, m + 352)
                left = jnp.dot(framed[rows, :256], wide[...], preferred_element_type=F32)
                right = jnp.dot(framed[rows, 256:], wide[...], preferred_element_type=F32)
                extra = border[v, rows]
                if g:
                    extra = pltpu.roll(extra, 128 - 32 * g, 1)
                held[g, rows, :128] = left[:, :128].astype(BF16)
                held[g, rows, 128:256] = (
                    left[:, 128:] + jnp.where(lane >= 118, extra, 0.0)
                ).astype(BF16)
                held[g, rows, 256:384] = (
                    right[:, :128] + jnp.where(lane < 10, extra, 0.0)
                ).astype(BF16)
                held[g, rows, 384:] = right[:, 128:].astype(BF16)
            save(b, g).start()
        return c

    lax.fori_loop(0, BASIS // 4, four, 0)
    for g in range(4):
        save(BASIS - 4 + g, g).wait()


def across_all(image, near, blocks, seam):
    return pl.pallas_call(
        across_body,
        out_shape=shape((BASIS, FRAMED, COLS), BF16),
        in_specs=[vmem()] * 4,
        out_specs=hbm(),
        scratch_shapes=[
            pltpu.VMEM((FRAMED, COLS), BF16),
            pltpu.VMEM((256, 256), BF16),
            pltpu.VMEM((3, FRAMED, 128), F32),
            pltpu.VMEM((4, FRAMED, COLS), BF16),
            pltpu.SemaphoreType.DMA((4,)),
        ],
        compiler_params=params(54),
        cost_estimate=cost(BASIS * FRAMED * COLS * COLS, 16 * 10**6),
        name="across",
    )(image, near, blocks, seam)


def solve(sums):
    total = jnp.sum(sums[...], axis=0)
    row, col = iota((16, 128), 0), iota((16, 128), 1)
    both = jnp.where(row < 8, total[0:1], total[1:2])
    both = jnp.where((col >> 4) == (row & 7), both, 0.0)
    for turn in (64, 32, 16):
        both = both + pltpu.roll(both, turn, 1)
    for k in range(BASIS):
        pivot = both[k : k + 1] / both[k : k + 1, k : k + 1]
        both = jnp.where(row == k, pivot, both - both[:, k : k + 1] * pivot)
    return both[:, BASIS : BASIS + 1]


def difference_body(
    sums, across_in, table_in, science_in, sigma, slot, coef_out, diff_out, leave_out,
    across, table, science, coef, bands, sems, save_sems,
):
    def load(i):
        first, _, span = BLOCKS[i]
        return pltpu.make_async_copy(
            across_in.at[:, pl.ds(first, span), :],
            across.at[i & 1, :, pl.ds(0, span), :],
            sems.at[i & 1],
        )

    load(0).start()
    table_load = pltpu.make_async_copy(table_in, table, sems.at[2])
    table_load.start()
    science_load = pltpu.make_async_copy(science_in, science, sems.at[3])
    science_load.start()
    found = solve(sums)
    coef[...] = jnp.broadcast_to(found, coef.shape)
    eye = iota((16, 128), 0) == iota((16, 128), 1)
    coef_out[...] = jnp.sum(jnp.where(eye, found, 0.0), axis=0, keepdims=True)
    scale = 1.0 / sigma[0]
    saves = []
    table_load.wait()
    for i, (first, rows, span) in enumerate(BLOCKS):
        load(i).wait()
        if i + 1 < len(BLOCKS):
            load(i + 1).start()
        for h in range(0, COLS, 256):
            model = None
            for b in range(BASIS):
                basis = jnp.dot(
                    table[b, :rows, :span],
                    across[i & 1, b, :span, h : h + 256],
                    preferred_element_type=F32,
                )
                term = coef[b : b + 1, :] * basis.astype(BF16).astype(F32)
                model = term if model is None else model + term
            if i == 0 and h == 0:
                science_load.wait()
            left = (science[first : first + rows, h : h + 256] - model) * scale
            bands[first // 8 : (first + rows) // 8, :, h : h + 256] = left.reshape(
                rows // 8, 8, 256
            ).astype(BF16)

        def send(band, c):
            pltpu.make_async_copy(
                bands.at[band], leave_out.at[slot[band]], save_sems.at[0]
            ).start()
            return c

        lax.fori_loop(first // 8, (first + rows) // 8, send, 0, unroll=4)
        some = pl.ds(first // 8, rows // 8)
        saves.append(pltpu.make_async_copy(bands.at[some], diff_out.at[some], save_sems.at[1 + i]))
        saves[-1].start()
    for save in saves:
        save.wait()
    pltpu.make_async_copy(bands, leave_out.at[pl.ds(0, ROWS // 8)], save_sems.at[0]).wait()


def difference_all(sums, across, table, science, sigma, slot, slots):
    return pl.pallas_call(
        difference_body,
        out_shape=(
            shape((1, 128), F32),
            shape((ROWS // 8, 8, COLS), BF16),
            shape((slots, 8, COLS), BF16),
        ),
        in_specs=[vmem()] + [hbm()] * 3 + [smem()] * 2,
        out_specs=(vmem(), hbm(), hbm()),
        scratch_shapes=[
            pltpu.VMEM((2, BASIS, SPAN, COLS), BF16),
            pltpu.VMEM((BASIS, STEP, SPAN), BF16),
            pltpu.VMEM((ROWS, COLS), F32),
            pltpu.VMEM((16, 256), F32),
            pltpu.VMEM((ROWS // 8, 8, COLS), BF16),
            pltpu.SemaphoreType.DMA((4,)),
            pltpu.SemaphoreType.DMA((1 + len(BLOCKS),)),
        ],
        compiler_params=params(54),
        name="difference",
    )(sums, across, table, science, sigma, slot)


def cut_body(diff, srow, scol, out, wide):
    wide[...] = diff[...].astype(F32).reshape(ROWS, COLS)
    row, lane = iota((32, 128), 0), iota((32, 128), 1)
    pick = (iota((8, 32), 1) >> 2 == iota((8, 32), 0)).astype(BF16)

    def cut(s, c):
        block = jnp.where(lane < 32, window(wide, srow[s], 32, scol[s]), 0.0)
        block = block + pltpu.roll(block, 32, 1)
        block = block + pltpu.roll(block, 64, 1)
        block = jnp.where((lane >> 5) == (row & 3), block, 0.0).astype(BF16)
        out[s] = jnp.dot(pick, block, preferred_element_type=F32).astype(BF16)
        return c

    lax.fori_loop(0, STAMPS, cut, 0)


def cut_stamps(diff, srow, scol):
    return pl.pallas_call(
        cut_body,
        out_shape=shape((STAMPS, 8, 128), BF16),
        in_specs=[vmem(), smem(), smem()],
        out_specs=vmem(),
        scratch_shapes=[pltpu.VMEM((ROWS, COLS), F32)],
        compiler_params=params(16),
        cost_estimate=cost(10**8, 3 * 10**6),
        name="cut_stamps",
    )(diff, srow, scol)


def smooth_body(landed, pick, blocks, out, patch, wide):
    fill_cols(wide, blocks)
    for first in range(0, ROWS, 256):

        def gather(m, c):
            pair = jnp.concatenate(
                [landed[pick[2 * m]].astype(F32), landed[pick[2 * m + 1]].astype(F32)], axis=0
            )
            patch[pl.ds(pl.multiple_of(m * 16, 16), 16)] = pair.astype(BF16)
            return c

        lax.fori_loop(first // 16, first // 16 + 16, gather, 0, unroll=4)
        out[first : first + 256] = jnp.dot(
            patch[first : first + 256], wide[...], preferred_element_type=F32
        ).astype(BF16)


def smooth(landed, pick, blocks):
    return pl.pallas_call(
        smooth_body,
        out_shape=shape((ROWS, COLS), BF16),
        in_specs=[vmem(), smem(), vmem()],
        out_specs=vmem(),
        scratch_shapes=[pltpu.VMEM((ROWS, COLS), BF16), pltpu.VMEM((COLS, COLS), BF16)],
        compiler_params=params(16),
        cost_estimate=cost(2 * ROWS * COLS * COLS, 3 * 10**6),
        name="smooth",
    )(landed, pick, blocks)


def fill_rows(table, blocks):
    table[:128, :128] = blocks[0]
    table[:128, 128:] = blocks[1]
    table[128:, :128] = jnp.zeros((STEP - 128, 128), BF16)
    table[128:, 128:] = blocks[0][: STEP - 128]


def filter_body(smoothed, near, cblocks, rblocks, out, framed, wide, table, tail):
    fill_cols(wide, cblocks)
    fill_rows(table, rblocks)
    tail[...] = jnp.concatenate(
        [near[...].astype(F32), jnp.zeros((8, COLS), F32)], axis=0
    ).astype(BF16)
    edge = jnp.dot(tail[...], wide[...], preferred_element_type=F32)
    edge = jnp.where(lax.axis_index("strip") == 0, edge, jnp.concatenate([edge[8:], edge[:8]], axis=0))
    frame(framed, smoothed, edge.astype(BF16))
    for first, rows, span in BLOCKS:
        out[first : first + rows] = jnp.dot(
            table[:rows, :span], framed[first : first + span], preferred_element_type=F32
        )


def filter_rows(smoothed, near, cblocks, rblocks):
    return pl.pallas_call(
        filter_body,
        out_shape=shape((ROWS, COLS), F32),
        in_specs=[vmem()] * 4,
        out_specs=vmem(),
        scratch_shapes=[
            pltpu.VMEM((FRAMED, COLS), BF16),
            pltpu.VMEM((COLS, COLS), BF16),
            pltpu.VMEM((STEP, SPAN), BF16),
            pltpu.VMEM((PAD, COLS), BF16),
        ],
        compiler_params=params(16),
        name="filter_rows",
    )(smoothed, near, cblocks, rblocks)


def shards(
    template, route_dest, route_row, kern_row, kern_col, science, noise_sigma,
    stamp_row, stamp_col, band_shift, psf_row, psf_col,
):
    ccds = lax.axis_size("ccd")
    devices = ccds * lax.axis_size("strip")
    bands = band_shift.shape[0]
    cap = 2 * bands // ccds
    outgoing = pack(route_dest, route_row, template, devices)
    arrived = lax.all_to_all(outgoing, BOTH, split_axis=0, concat_axis=0, tiled=True)
    cols, rows, pcols, prows, stamp_table, krl, seam, slot, pick, sky = tables(
        kern_row, kern_col, psf_row, psf_col, band_shift, stamp_row, stamp_col, science
    )
    image, edge = coadd(arrived, stamp_table)
    near = lax.ppermute(edge, "strip", SWAP)
    sums = stamp_sums(
        image, near, noise_sigma, stamp_row, stamp_col, stamp_table, krl, sky, devices
    )
    sums = lax.all_to_all(sums, BOTH, split_axis=0, concat_axis=0, tiled=True)
    across = across_all(image, near, cols, seam)
    coef, diff, leaving = difference_all(
        sums, across, rows, science, noise_sigma, slot, ccds * cap
    )
    landed = lax.all_to_all(
        leaving.reshape(ccds, cap, 8, COLS), "ccd", split_axis=0, concat_axis=0, tiled=True
    ).reshape(ccds * cap, 8, COLS)
    stamp_cut = cut_stamps(diff, stamp_row, stamp_col).reshape(STAMPS, 1024)
    last = jnp.where(lax.axis_index("strip") == 0, pick[bands - 1], pick[0])
    beside = lax.ppermute(
        lax.dynamic_slice(landed, (last, 0, 0), (1, 8, COLS))[0], "strip", SWAP
    )
    smoothed = smooth(landed, pick, pcols)
    filtered = filter_rows(smoothed, beside, pcols, prows)
    return (diff.reshape(ROWS, COLS), stamp_cut, coef[0, :BASIS], filtered)


def solution(mesh):
    placed = (
        P(BOTH, None, None), P(BOTH), P(BOTH), P(), P(), P(BOTH, None),
        P(BOTH), P(BOTH), P(BOTH), P(), P(), P(),
    )
    return jax.shard_map(
        shards,
        mesh=mesh,
        in_specs=placed,
        out_specs=(P(BOTH, None), P(BOTH, None), P(), P(BOTH, None)),
        check_vma=False,
    )
```

```python
import jax
import jax.numpy as jnp
from jax import lax
from jax.experimental import pallas as pl
from jax.experimental.pallas import tpu as pltpu
from jax.sharding import PartitionSpec as P

BASIS = 12
KTAPS = 21
PSF_TAPS = 15
STAMPS = 16
ROWS = 1024
COLS = 512
PAD = 16
FRAMED = ROWS + 2 * PAD
STEP = 224
SPAN = 256
WIN = 64
LANES = BASIS * 32
LARGE = 58
BOTH = ("ccd", "strip")
SWAP = [(0, 1), (1, 0)]
F32 = jnp.float32
BF16 = jnp.bfloat16
I32 = jnp.int32
HIGH = lax.Precision.HIGHEST

BLOCKS = [(j, min(STEP, ROWS - j), min(SPAN, FRAMED - j)) for j in range(0, ROWS, STEP)]


def vmem():
    return pl.BlockSpec(memory_space=pltpu.VMEM)


def hbm():
    return pl.BlockSpec(memory_space=pltpu.HBM)


def smem():
    return pl.BlockSpec(memory_space=pltpu.SMEM)


def params(mib):
    return pltpu.CompilerParams(vmem_limit_bytes=mib * 2**20)


def iota(shape, dim):
    return lax.broadcasted_iota(I32, shape, dim)


def shape(dims, dtype):
    return jax.ShapeDtypeStruct(dims, dtype)


def cost(flops, moved):
    return pl.CostEstimate(flops=flops, bytes_accessed=moved, transcendentals=0)


CHUNKS = 8


def pack_body(dest_in, row_in, pieces_in, sent, dest, row, pieces, out, count, rows, sems):
    devices = out.shape[0]
    loads = [
        pltpu.make_async_copy(src, dst, sems.at[CHUNKS + i])
        for i, (src, dst) in enumerate([(dest_in, dest), (row_in, row), (pieces_in, pieces)])
    ]
    for load in loads:
        load.start()
    out[...] = jnp.zeros(out.shape, out.dtype)

    def clear(d, c):
        count[d] = 0
        rows[2 * d] = 4096
        rows[2 * d + 1] = 4096
        return c

    lax.fori_loop(0, devices, clear, 0, unroll=8)
    for load in loads:
        load.wait()

    def place(i, c):
        d = dest[i]
        k = count[d]
        count[d] = k + 1
        rows[2 * d + k] = row[i]
        piece = pieces[i]
        for q in range(4):
            out[d, 4 * k + q] = piece[:, 128 * q : 128 * (q + 1)]
        return c

    lax.fori_loop(0, pieces.shape[0], place, 0, unroll=8)
    sub, lane = iota((8, 128), 0), iota((8, 128), 1)

    def tell(d, c):
        target = jnp.where(lane < 64, rows[2 * d], rows[2 * d + 1]) + sub
        told = jnp.where((lane & 32) == 0, target >> 5, target & 31)
        out[d, 8] = told.astype(F32).astype(BF16)
        return c

    part = devices // CHUNKS
    sends = []
    for i in range(CHUNKS):
        lax.fori_loop(i * part, (i + 1) * part, tell, 0, unroll=8)
        some = pl.ds(i * part, part)
        sends.append(pltpu.make_async_copy(out.at[some], sent.at[some], sems.at[i]))
        sends[-1].start()
    for send in sends:
        send.wait()


def pack(route_dest, route_row, template, devices):
    pieces = template.shape[0]
    return pl.pallas_call(
        pack_body,
        out_shape=shape((devices, 9, 8, 128), BF16),
        in_specs=[hbm()] * 3,
        out_specs=hbm(),
        scratch_shapes=[
            pltpu.SMEM((pieces,), I32),
            pltpu.SMEM((pieces,), I32),
            pltpu.VMEM(template.shape, BF16),
            pltpu.VMEM((devices, 9, 8, 128), BF16),
            pltpu.SMEM((devices,), I32),
            pltpu.SMEM((2 * devices,), I32),
            pltpu.SemaphoreType.DMA((CHUNKS + 3,)),
        ],
        compiler_params=params(LARGE),
        name="pack",
    )(route_dest, route_row, template)


def band_table(taps, count, size, offset):
    lag = iota((128, 128), 0) - iota((128, 128), 1) + offset
    table = jnp.zeros((128, 128), F32)
    for t in range(count):
        if -127 <= t - offset <= 127:
            table = jnp.where(lag == t, taps(t), table)
    return table.astype(BF16)


def window(ref, first_row, rows, first_col):
    tile = jnp.minimum(jnp.maximum(first_col, 0) >> 7, 2) * 128
    top = jnp.minimum((first_row >> 3) * 8, ref.shape[0] - rows - 8)
    block = ref[pl.ds(pl.multiple_of(top, 8), rows + 8), pl.ds(pl.multiple_of(tile, 128), 256)]
    turn = (256 - (first_col - tile)) & 255
    block = pltpu.roll(block, turn, 1)[:, :128]
    return pltpu.roll(block, lax.rem(rows + 8 - (first_row - top), rows + 8), 0)[:rows]


def tables_body(
    kr, kc, pr, pc, kcl, shift, srow, scol, science,
    cols_out, rows_out, pcols_out, prows_out, stamp_out, ready_out, down_out, seam_out,
    slot_out, pick_out, sky_out, count,
):
    for b in range(BASIS):
        for k in range(3):
            cols_out[b, k] = band_table(lambda t: kc[b, t], KTAPS, 128, 10 + 128 * (k - 1))
        for k in range(2):
            lag = iota((128, 128), 1) - iota((128, 128), 0) - 6 + 128 * k
            table = jnp.zeros((128, 128), F32)
            for t in range(KTAPS):
                table = jnp.where(lag == t, kr[b, t], table)
            table = table.astype(BF16)
            rows_out[b, :128, 128 * k : 128 * k + 128] = table
            if k == 0:
                rows_out[b, 128:, 128:] = table[: STEP - 128]
                rows_out[b, 128:, :128] = jnp.zeros((STEP - 128, 128), BF16)
    for k in range(3):
        pcols_out[k] = band_table(lambda t: pc[t], PSF_TAPS, 128, 7 + 128 * (k - 1))
    for k in range(2):
        lag = iota((128, 128), 1) - iota((128, 128), 0) - 9 + 128 * k
        table = jnp.zeros((128, 128), F32)
        for t in range(PSF_TAPS):
            table = jnp.where(lag == t, pr[t], table)
        prows_out[k] = table.astype(BF16)
    lag = iota((128, LANES), 0) - (iota((128, LANES), 1) & 31)
    table = jnp.zeros((128, LANES), F32)
    for t in range(KTAPS):
        table = jnp.where(lag == t, kcl[t : t + 1, :], table)
    stamp_out[...] = table.astype(BF16)
    ready_out[...] = jnp.zeros(ready_out.shape, F32)
    for q in range(3):
        for g in range(4):
            lag = iota((32, 64), 1) - iota((32, 64), 0)
            table = jnp.zeros((32, 64), F32)
            for t in range(KTAPS):
                table = jnp.where(lag == t, kr[4 * q + g, t], table)
            down_out[q, 32 * g : 32 * g + 32] = table.astype(BF16)
    seam_out[...] = jnp.zeros(seam_out.shape, BF16)
    place = ((iota((32, 128), 1) + 16) & 31) - 16
    source = iota((32, 128), 0) - 16
    crosses = (place >= -10) & (place < 10) & ((place < 0) != (source < 0))
    lag = jnp.where(crosses, source - place + 10, -1)
    for v in range(3):
        taps = pltpu.roll(kcl[:, 128 * v : 128 * v + 128], 112, 1)
        table = jnp.zeros((32, 128), F32)
        for t in range(KTAPS):
            table = jnp.where(lag == t, taps[t : t + 1, :], table)
        seam_out[112:144, 128 * v : 128 * v + 128] = table.astype(BF16)

    own, ccds = lax.axis_index("ccd"), lax.axis_size("ccd")
    cap = slot_out.shape[0] * 2 // ccds

    def clear(v, c):
        count[v] = 0
        return c

    lax.fori_loop(0, ccds, clear, 0)

    def seat(m, c):
        v = shift[m]
        k = count[v]
        count[v] = k + 1
        slot_out[m] = lax.rem(own + v, ccds) * cap + k
        pick_out[m] = lax.rem(own - v + ccds, ccds) * cap + k
        return c

    lax.fori_loop(0, slot_out.shape[0], seat, 0)
    lane = iota((32, 128), 1)

    def cut(s, c):
        sky = jnp.where(lane < 32, window(science, srow[s], 32, scol[s]), 0.0)
        sky = sky + pltpu.roll(sky, 32, 1)
        sky_out[s] = sky + pltpu.roll(sky, 64, 1)
        return c

    lax.fori_loop(0, STAMPS, cut, 0)


def tables(kern_row, kern_col, psf_row, psf_col, band_shift, stamp_row, stamp_col, science):
    kc = kern_col.astype(F32)
    expand = lambda taps: jnp.pad(jnp.repeat(taps.T, 32, axis=1), ((0, 3), (0, 0)))
    return pl.pallas_call(
        tables_body,
        out_shape=(
            shape((BASIS, 3, 128, 128), BF16),
            shape((BASIS, STEP, SPAN), BF16),
            shape((3, 128, 128), BF16),
            shape((2, 128, 128), BF16),
            shape((128, LANES), BF16),
            shape((8, 128), F32),
            shape((3, 128, WIN), BF16),
            shape((256, LANES), BF16),
            shape(band_shift.shape, I32),
            shape(band_shift.shape, I32),
            shape((STAMPS, 32, 128), F32),
        ),
        in_specs=[smem()] * 4 + [vmem()] + [smem()] * 3 + [vmem()],
        out_specs=(vmem(),) * 8 + (smem(),) * 2 + (vmem(),),
        scratch_shapes=[pltpu.SMEM((64,), I32)],
        compiler_params=params(16),
        cost_estimate=cost(2 * 10**9, 4 * 10**6),
        name="tables",
    )(
        kern_row.astype(F32), kc, psf_row.astype(F32), psf_col.astype(F32),
        expand(kc),
        band_shift, stamp_row, stamp_col, science,
    )


def coadd_body(arrived, ready, out, edge, held):
    senders = arrived.shape[0]
    half = senders * 8
    told = arrived[:, 8].astype(F32).reshape(half, 128).T
    target = jnp.concatenate(
        [told[64 * k : 64 * k + 1] * 32.0 + told[64 * k + 32 : 64 * k + 33] for k in range(2)], axis=1
    ).astype(I32)
    for k in range(2):
        for q in range(4):
            part = arrived[:, 4 * k + q].astype(F32).reshape(half, 128)
            held[half * k : half * (k + 1), 128 * q : 128 * (q + 1)] = part.astype(BF16)
    for m in range(0, ROWS, 256):
        hit = (iota((256, 2 * half), 0) + m) == target
        placer = jnp.where(hit, 1.0, 0.0).astype(BF16)
        out[m : m + 256] = jnp.dot(placer, held[...], preferred_element_type=F32).astype(BF16)
    strip = lax.axis_index("strip")

    @pl.when(strip == 0)
    def _():
        edge[...] = out[ROWS - PAD :]

    @pl.when(strip != 0)
    def _():
        edge[...] = out[:PAD]


def coadd(arrived, ready):
    senders = arrived.shape[0]
    return pl.pallas_call(
        coadd_body,
        out_shape=(shape((ROWS, COLS), BF16), shape((PAD, COLS), BF16)),
        in_specs=[vmem(), vmem()],
        out_specs=(vmem(), vmem()),
        scratch_shapes=[pltpu.VMEM((senders * 16, COLS), BF16)],
        compiler_params=params(16),
        name="coadd",
    )(arrived, ready)


def frame(framed, image, near):
    strip = lax.axis_index("strip")
    rows = near[...].astype(F32)
    framed[PAD : PAD + ROWS] = image[...].astype(framed.dtype)
    framed[:PAD] = jnp.where(strip == 0, 0.0, rows).astype(framed.dtype)
    framed[PAD + ROWS :] = jnp.where(strip == 0, rows, 0.0).astype(framed.dtype)


def stamps_body(image, near, sigma, srow, scol, table, down, sky, out, framed, wins, across, basis):
    frame(framed, image, near)
    lane = iota((WIN, 128), 1)

    def cut(s, c):
        first = scol[s] - 10
        block = window(framed, srow[s] + 6, WIN, first)
        inside = (lane < 52) & (lane + first >= 0) & (lane + first < COLS)
        wins[s] = jnp.where(inside, block, 0.0).astype(BF16)
        return c

    lax.fori_loop(0, STAMPS, cut, 0, unroll=2)
    wide = jnp.dot(
        wins[...].reshape(STAMPS * WIN, 128), table[...], preferred_element_type=F32
    )
    across[...] = wide.astype(BF16).reshape(STAMPS, WIN, LANES)
    group = iota((32, 128), 1) >> 5

    def rows(s, total):
        parts = []
        for q in range(3):
            every = jnp.dot(
                down[q], across[s, :, 128 * q : 128 * q + 128], preferred_element_type=F32
            )
            acc = every[:32]
            for g in range(1, 4):
                acc = jnp.where(group == g, every[32 * g : 32 * g + 32], acc)
            done = acc.astype(BF16)
            basis[pl.ds(pl.multiple_of(s * 32, 32), 32), 128 * q : 128 * q + 128] = done
            parts.append(total[q] + jnp.sum(done.astype(F32) * sky[s], axis=0, keepdims=True))
        return tuple(parts)

    total = lax.fori_loop(
        0, STAMPS, rows, tuple(jnp.zeros((1, 128), F32) for _ in range(3)), unroll=4
    )
    total = jnp.concatenate(total, axis=1)
    pairs = lax.dot_general(
        basis[...], basis[...], (((0,), (0,)), ((), ())), preferred_element_type=F32
    )
    same = (iota((LANES, LANES), 0) & 31) == (iota((LANES, LANES), 1) & 31)
    pairs = jnp.where(same, pairs, 0.0)
    gram = [jnp.sum(pairs[32 * b : 32 * b + 32], axis=0, keepdims=True) for b in range(BASIS)]
    gram = jnp.concatenate(gram + [total, jnp.zeros((3, LANES), F32)], axis=0)
    parts = []
    for q in range(3):
        part = gram[:, 128 * q : 128 * q + 128]
        for turn in (1, 2, 4, 8, 16):
            part = part + pltpu.roll(part, 128 - turn, 1)
        parts.append(part)
    row, col = iota((16, 128), 0), iota((16, 128), 1)
    both = jnp.zeros((16, 128), F32)
    goal = jnp.zeros((16, 1), F32)
    for b in range(BASIS):
        entry = parts[b // 4][:, 32 * (b & 3) : 32 * (b & 3) + 1]
        both = jnp.where((col & 15) == b, entry, both)
        goal = jnp.where(row[:, :1] == b, entry[BASIS : BASIS + 1], goal)
    both = jnp.where((col & 15) == BASIS, goal, both)
    both = jnp.where(((col >> 4) == (row & 7)) & (row < BASIS), both, 0.0)
    both = both / (sigma[0] * sigma[0])
    packed = jnp.concatenate(
        [jnp.sum(both[:8], axis=0, keepdims=True), jnp.sum(both[8:], axis=0, keepdims=True)], axis=0
    )
    out[...] = jnp.broadcast_to(packed[None], out.shape)


def stamp_sums(image, near, sigma, srow, scol, table, down, sky, devices):
    return pl.pallas_call(
        stamps_body,
        out_shape=shape((devices, 2, 128), F32),
        in_specs=[vmem(), vmem(), smem(), smem(), smem(), vmem(), vmem(), vmem()],
        out_specs=vmem(),
        scratch_shapes=[
            pltpu.VMEM((FRAMED, COLS), F32),
            pltpu.VMEM((STAMPS, WIN, 128), BF16),
            pltpu.VMEM((STAMPS, WIN, LANES), BF16),
            pltpu.VMEM((STAMPS * 32, LANES), BF16),
        ],
        compiler_params=params(16),
        name="stamp_sums",
    )(image, near, sigma, srow, scol, table, down, sky)


def fill_cols(wide, blocks):
    for i in range(4):
        for o in range(4):
            if abs(i - o) <= 1:
                wide[128 * i : 128 * i + 128, 128 * o : 128 * o + 128] = blocks[i - o + 1]
            else:
                wide[128 * i : 128 * i + 128, 128 * o : 128 * o + 128] = jnp.zeros((128, 128), BF16)


def across_body(image, near, blocks, seam, out, framed, wide, border, held, sems):
    frame(framed, image, near)
    for m in range(0, FRAMED, 352):
        for v in range(3):
            border[v, m : m + 352] = jnp.dot(
                framed[m : m + 352, 128:384],
                seam[:, 128 * v : 128 * v + 128],
                preferred_element_type=F32,
            )
    lane = iota((352, 128), 1)

    def save(b, g):
        return pltpu.make_async_copy(held.at[g], out.at[b], sems.at[g])

    def four(v, c):
        for g in range(4):
            b = 4 * v + g
            for i in range(2):
                for o in range(2):
                    wide[128 * i : 128 * i + 128, 128 * o : 128 * o + 128] = blocks[b, i - o + 1]

            @pl.when(v > 0)
            def _():
                save(b - 4, g).wait()

            for m in range(0, FRAMED, 352):
                rows = slice(m, m + 352)
                left = jnp.dot(framed[rows, :256], wide[...], preferred_element_type=F32)
                right = jnp.dot(framed[rows, 256:], wide[...], preferred_element_type=F32)
                extra = border[v, rows]
                if g:
                    extra = pltpu.roll(extra, 128 - 32 * g, 1)
                held[g, rows, :128] = left[:, :128].astype(BF16)
                held[g, rows, 128:256] = (
                    left[:, 128:] + jnp.where(lane >= 118, extra, 0.0)
                ).astype(BF16)
                held[g, rows, 256:384] = (
                    right[:, :128] + jnp.where(lane < 10, extra, 0.0)
                ).astype(BF16)
                held[g, rows, 384:] = right[:, 128:].astype(BF16)
            save(b, g).start()
        return c

    lax.fori_loop(0, BASIS // 4, four, 0)
    for g in range(4):
        save(BASIS - 4 + g, g).wait()


def across_all(image, near, blocks, seam):
    return pl.pallas_call(
        across_body,
        out_shape=shape((BASIS, FRAMED, COLS), BF16),
        in_specs=[vmem()] * 4,
        out_specs=hbm(),
        scratch_shapes=[
            pltpu.VMEM((FRAMED, COLS), BF16),
            pltpu.VMEM((256, 256), BF16),
            pltpu.VMEM((3, FRAMED, 128), F32),
            pltpu.VMEM((4, FRAMED, COLS), BF16),
            pltpu.SemaphoreType.DMA((4,)),
        ],
        compiler_params=params(54),
        cost_estimate=cost(BASIS * FRAMED * COLS * COLS, 16 * 10**6),
        name="across",
    )(image, near, blocks, seam)


def solve(sums):
    total = jnp.sum(sums[...], axis=0)
    row, col = iota((16, 128), 0), iota((16, 128), 1)
    both = jnp.where(row < 8, total[0:1], total[1:2])
    both = jnp.where((col >> 4) == (row & 7), both, 0.0)
    for turn in (64, 32, 16):
        both = both + pltpu.roll(both, turn, 1)
    for k in range(BASIS):
        pivot = both[k : k + 1] / both[k : k + 1, k : k + 1]
        both = jnp.where(row == k, pivot, both - both[:, k : k + 1] * pivot)
    return both[:, BASIS : BASIS + 1]


def difference_body(
    across_in, sums_in, sigma_in, slot_in, table, science, coef_out, diff_out, leave_out,
    across, sums, sigma, slot, coef, bands, sems, save_sems,
):
    def load(i):
        first, _, span = BLOCKS[i]
        return pltpu.make_async_copy(
            across_in.at[:, pl.ds(first, span), :],
            across.at[i & 1, :, pl.ds(0, span), :],
            sems.at[i & 1],
        )

    small = [
        pltpu.make_async_copy(src, dst, sems.at[2 + i])
        for i, (src, dst) in enumerate([(sums_in, sums), (sigma_in, sigma), (slot_in, slot)])
    ]
    for one in small:
        one.start()
    load(0).start()
    for one in small:
        one.wait()
    found = solve(sums)
    coef[...] = jnp.broadcast_to(found, coef.shape)
    eye = iota((16, 128), 0) == iota((16, 128), 1)
    coef_out[...] = jnp.sum(jnp.where(eye, found, 0.0), axis=0, keepdims=True)
    scale = 1.0 / sigma[0]
    saves = []
    for i, (first, rows, span) in enumerate(BLOCKS):
        if i + 1 < len(BLOCKS):
            load(i + 1).start()
        load(i).wait()
        for h in range(0, COLS, 256):
            model = None
            for b in range(BASIS):
                basis = jnp.dot(
                    table[b, :rows, :span],
                    across[i & 1, b, :span, h : h + 256],
                    preferred_element_type=F32,
                )
                term = coef[b : b + 1, :] * basis.astype(BF16).astype(F32)
                model = term if model is None else model + term
            left = (science[first : first + rows, h : h + 256] - model) * scale
            bands[first // 8 : (first + rows) // 8, :, h : h + 256] = left.reshape(
                rows // 8, 8, 256
            ).astype(BF16)

        def send(band, c):
            pltpu.make_async_copy(
                bands.at[band], leave_out.at[slot[band]], save_sems.at[0]
            ).start()
            return c

        lax.fori_loop(first // 8, (first + rows) // 8, send, 0, unroll=4)
        some = pl.ds(first // 8, rows // 8)
        saves.append(pltpu.make_async_copy(bands.at[some], diff_out.at[some], save_sems.at[1 + i]))
        saves[-1].start()
    for save in saves:
        save.wait()
    pltpu.make_async_copy(bands, leave_out.at[pl.ds(0, ROWS // 8)], save_sems.at[0]).wait()


def difference_all(sums, across, table, science, sigma, slot, slots):
    return pl.pallas_call(
        difference_body,
        out_shape=(
            shape((1, 128), F32),
            shape((ROWS // 8, 8, COLS), BF16),
            shape((slots, 8, COLS), BF16),
        ),
        in_specs=[hbm()] * 4 + [vmem()] * 2,
        out_specs=(vmem(), hbm(), hbm()),
        scratch_shapes=[
            pltpu.VMEM((2, BASIS, SPAN, COLS), BF16),
            pltpu.VMEM(sums.shape, F32),
            pltpu.SMEM((1,), F32),
            pltpu.SMEM(slot.shape, I32),
            pltpu.VMEM((16, 256), F32),
            pltpu.VMEM((ROWS // 8, 8, COLS), BF16),
            pltpu.SemaphoreType.DMA((5,)),
            pltpu.SemaphoreType.DMA((1 + len(BLOCKS),)),
        ],
        compiler_params=params(48),
        name="difference",
    )(across, sums, sigma, slot, table, science)


def cut_body(diff, srow, scol, out, wide):
    wide[...] = diff[...].astype(F32).reshape(ROWS, COLS)
    row, lane = iota((32, 128), 0), iota((32, 128), 1)
    pick = (iota((8, 32), 1) >> 2 == iota((8, 32), 0)).astype(BF16)

    def cut(s, c):
        block = jnp.where(lane < 32, window(wide, srow[s], 32, scol[s]), 0.0)
        block = block + pltpu.roll(block, 32, 1)
        block = block + pltpu.roll(block, 64, 1)
        block = jnp.where((lane >> 5) == (row & 3), block, 0.0).astype(BF16)
        out[s] = jnp.dot(pick, block, preferred_element_type=F32).astype(BF16)
        return c

    lax.fori_loop(0, STAMPS, cut, 0)


def cut_stamps(diff, srow, scol):
    return pl.pallas_call(
        cut_body,
        out_shape=shape((STAMPS, 8, 128), BF16),
        in_specs=[vmem(), smem(), smem()],
        out_specs=vmem(),
        scratch_shapes=[pltpu.VMEM((ROWS, COLS), F32)],
        compiler_params=params(16),
        cost_estimate=cost(10**8, 3 * 10**6),
        name="cut_stamps",
    )(diff, srow, scol)


def smooth_body(landed, pick, blocks, out, patch, wide):
    fill_cols(wide, blocks)
    for first in range(0, ROWS, 256):

        def gather(m, c):
            pair = jnp.concatenate(
                [landed[pick[2 * m]].astype(F32), landed[pick[2 * m + 1]].astype(F32)], axis=0
            )
            patch[pl.ds(pl.multiple_of(m * 16, 16), 16)] = pair.astype(BF16)
            return c

        lax.fori_loop(first // 16, first // 16 + 16, gather, 0, unroll=4)
        out[first : first + 256] = jnp.dot(
            patch[first : first + 256], wide[...], preferred_element_type=F32
        ).astype(BF16)


def smooth(landed, pick, blocks):
    return pl.pallas_call(
        smooth_body,
        out_shape=shape((ROWS, COLS), BF16),
        in_specs=[vmem(), smem(), vmem()],
        out_specs=vmem(),
        scratch_shapes=[pltpu.VMEM((ROWS, COLS), BF16), pltpu.VMEM((COLS, COLS), BF16)],
        compiler_params=params(16),
        cost_estimate=cost(2 * ROWS * COLS * COLS, 3 * 10**6),
        name="smooth",
    )(landed, pick, blocks)


def fill_rows(table, blocks):
    table[:128, :128] = blocks[0]
    table[:128, 128:] = blocks[1]
    table[128:, :128] = jnp.zeros((STEP - 128, 128), BF16)
    table[128:, 128:] = blocks[0][: STEP - 128]


def filter_body(smoothed, near, cblocks, rblocks, out, framed, wide, table, tail):
    fill_cols(wide, cblocks)
    fill_rows(table, rblocks)
    tail[...] = jnp.concatenate(
        [near[...].astype(F32), jnp.zeros((8, COLS), F32)], axis=0
    ).astype(BF16)
    edge = jnp.dot(tail[...], wide[...], preferred_element_type=F32)
    edge = jnp.where(lax.axis_index("strip") == 0, edge, jnp.concatenate([edge[8:], edge[:8]], axis=0))
    frame(framed, smoothed, edge.astype(BF16))
    for first, rows, span in BLOCKS:
        out[first : first + rows] = jnp.dot(
            table[:rows, :span], framed[first : first + span], preferred_element_type=F32
        )


def filter_rows(smoothed, near, cblocks, rblocks):
    return pl.pallas_call(
        filter_body,
        out_shape=shape((ROWS, COLS), F32),
        in_specs=[vmem()] * 4,
        out_specs=vmem(),
        scratch_shapes=[
            pltpu.VMEM((FRAMED, COLS), BF16),
            pltpu.VMEM((COLS, COLS), BF16),
            pltpu.VMEM((STEP, SPAN), BF16),
            pltpu.VMEM((PAD, COLS), BF16),
        ],
        compiler_params=params(16),
        name="filter_rows",
    )(smoothed, near, cblocks, rblocks)


def shards(
    template, route_dest, route_row, kern_row, kern_col, science, noise_sigma,
    stamp_row, stamp_col, band_shift, psf_row, psf_col,
):
    ccds = lax.axis_size("ccd")
    devices = ccds * lax.axis_size("strip")
    bands = band_shift.shape[0]
    cap = 2 * bands // ccds
    outgoing = pack(route_dest, route_row, template, devices)
    arrived = lax.all_to_all(outgoing, BOTH, split_axis=0, concat_axis=0, tiled=True)
    cols, rows, pcols, prows, stamp_table, ready, down, seam, slot, pick, sky = tables(
        kern_row, kern_col, psf_row, psf_col, band_shift, stamp_row, stamp_col, science
    )
    image, edge = coadd(arrived, ready)
    near = lax.ppermute(edge, "strip", SWAP)
    sums = stamp_sums(
        image, near, noise_sigma, stamp_row, stamp_col, stamp_table, down, sky, devices
    )
    sums = lax.all_to_all(sums, BOTH, split_axis=0, concat_axis=0, tiled=True)
    across = across_all(image, near, cols, seam)
    coef, diff, leaving = difference_all(
        sums, across, rows, science, noise_sigma, slot, ccds * cap
    )
    landed = lax.all_to_all(
        leaving.reshape(ccds, cap, 8, COLS), "ccd", split_axis=0, concat_axis=0, tiled=True
    ).reshape(ccds * cap, 8, COLS)
    stamp_cut = cut_stamps(diff, stamp_row, stamp_col).reshape(STAMPS, 1024)
    last = jnp.where(lax.axis_index("strip") == 0, pick[bands - 1], pick[0])
    beside = lax.ppermute(
        lax.dynamic_slice(landed, (last, 0, 0), (1, 8, COLS))[0], "strip", SWAP
    )
    smoothed = smooth(landed, pick, pcols)
    filtered = filter_rows(smoothed, beside, pcols, prows)
    return (diff.reshape(ROWS, COLS), stamp_cut, coef[0, :BASIS], filtered)


def solution(mesh):
    placed = (
        P(BOTH, None, None), P(BOTH), P(BOTH), P(), P(), P(BOTH, None),
        P(BOTH), P(BOTH), P(BOTH), P(), P(), P(),
    )
    return jax.shard_map(
        shards,
        mesh=mesh,
        in_specs=placed,
        out_specs=(P(BOTH, None), P(BOTH, None), P(), P(BOTH, None)),
        check_vma=False,
    )
```

```python
import jax
import jax.numpy as jnp
from jax import lax
from jax.experimental import pallas as pl
from jax.experimental.pallas import tpu as pltpu
from jax.sharding import PartitionSpec as P

BASIS = 12
KTAPS = 21
PSF_TAPS = 15
STAMPS = 16
ROWS = 1024
COLS = 512
PAD = 16
FRAMED = ROWS + 2 * PAD
STEP = 224
SPAN = 256
WIN = 64
LANES = BASIS * 32
LARGE = 58
BOTH = ("ccd", "strip")
SWAP = [(0, 1), (1, 0)]
F32 = jnp.float32
BF16 = jnp.bfloat16
I32 = jnp.int32
HIGH = lax.Precision.HIGHEST

BLOCKS = [(j, min(STEP, ROWS - j), min(SPAN, FRAMED - j)) for j in range(0, ROWS, STEP)]


def vmem():
    return pl.BlockSpec(memory_space=pltpu.VMEM)


def hbm():
    return pl.BlockSpec(memory_space=pltpu.HBM)


def smem():
    return pl.BlockSpec(memory_space=pltpu.SMEM)


def params(mib):
    return pltpu.CompilerParams(vmem_limit_bytes=mib * 2**20)


def iota(shape, dim):
    return lax.broadcasted_iota(I32, shape, dim)


def shape(dims, dtype):
    return jax.ShapeDtypeStruct(dims, dtype)


def cost(flops, moved):
    return pl.CostEstimate(flops=flops, bytes_accessed=moved, transcendentals=0)


CHUNKS = 8


def pack_body(dest_in, row_in, pieces_in, sent, dest, row, pieces, out, count, rows, sems):
    devices = out.shape[0]
    loads = [
        pltpu.make_async_copy(src, dst, sems.at[CHUNKS + i])
        for i, (src, dst) in enumerate([(dest_in, dest), (row_in, row), (pieces_in, pieces)])
    ]
    for load in loads:
        load.start()
    out[...] = jnp.zeros(out.shape, out.dtype)

    def clear(d, c):
        count[d] = 0
        rows[2 * d] = 4096
        rows[2 * d + 1] = 4096
        return c

    lax.fori_loop(0, devices, clear, 0, unroll=8)
    for load in loads:
        load.wait()

    def place(i, c):
        d = dest[i]
        k = count[d]
        count[d] = k + 1
        rows[2 * d + k] = row[i]
        piece = pieces[i]
        for q in range(4):
            out[d, 4 * k + q] = piece[:, 128 * q : 128 * (q + 1)]
        return c

    lax.fori_loop(0, pieces.shape[0], place, 0, unroll=8)
    sub, lane = iota((8, 128), 0), iota((8, 128), 1)

    def tell(d, c):
        target = jnp.where(lane < 64, rows[2 * d], rows[2 * d + 1]) + sub
        told = jnp.where((lane & 32) == 0, target >> 5, target & 31)
        out[d, 8] = told.astype(F32).astype(BF16)
        return c

    part = devices // CHUNKS
    sends = []
    for i in range(CHUNKS):
        lax.fori_loop(i * part, (i + 1) * part, tell, 0, unroll=8)
        some = pl.ds(i * part, part)
        sends.append(pltpu.make_async_copy(out.at[some], sent.at[some], sems.at[i]))
        sends[-1].start()
    for send in sends:
        send.wait()


def pack(route_dest, route_row, template, devices):
    pieces = template.shape[0]
    return pl.pallas_call(
        pack_body,
        out_shape=shape((devices, 9, 8, 128), BF16),
        in_specs=[hbm()] * 3,
        out_specs=hbm(),
        scratch_shapes=[
            pltpu.SMEM((pieces,), I32),
            pltpu.SMEM((pieces,), I32),
            pltpu.VMEM(template.shape, BF16),
            pltpu.VMEM((devices, 9, 8, 128), BF16),
            pltpu.SMEM((devices,), I32),
            pltpu.SMEM((2 * devices,), I32),
            pltpu.SemaphoreType.DMA((CHUNKS + 3,)),
        ],
        compiler_params=params(LARGE),
        name="pack",
    )(route_dest, route_row, template)


def band_table(taps, count, size, offset):
    lag = iota((128, 128), 0) - iota((128, 128), 1) + offset
    table = jnp.zeros((128, 128), F32)
    for t in range(count):
        if -127 <= t - offset <= 127:
            table = jnp.where(lag == t, taps(t), table)
    return table.astype(BF16)


def window(ref, first_row, rows, first_col):
    tile = jnp.minimum(jnp.maximum(first_col, 0) >> 7, 2) * 128
    top = jnp.minimum((first_row >> 3) * 8, ref.shape[0] - rows - 8)
    block = ref[pl.ds(pl.multiple_of(top, 8), rows + 8), pl.ds(pl.multiple_of(tile, 128), 256)]
    turn = (256 - (first_col - tile)) & 255
    block = pltpu.roll(block, turn, 1)[:, :128]
    return pltpu.roll(block, lax.rem(rows + 8 - (first_row - top), rows + 8), 0)[:rows]


def tables_body(
    kr, kc, pr, pc, kcl, shift, srow, scol, science,
    cols_out, rows_out, pcols_out, prows_out, stamp_out, ready_out, down_out, seam_out,
    slot_out, pick_out, sky_out, count,
):
    for b in range(BASIS):
        for k in range(3):
            cols_out[b, k] = band_table(lambda t: kc[b, t], KTAPS, 128, 10 + 128 * (k - 1))
        for k in range(2):
            lag = iota((128, 128), 1) - iota((128, 128), 0) - 6 + 128 * k
            table = jnp.zeros((128, 128), F32)
            for t in range(KTAPS):
                table = jnp.where(lag == t, kr[b, t], table)
            table = table.astype(BF16)
            rows_out[b, :128, 128 * k : 128 * k + 128] = table
            if k == 0:
                rows_out[b, 128:, 128:] = table[: STEP - 128]
                rows_out[b, 128:, :128] = jnp.zeros((STEP - 128, 128), BF16)
    for k in range(3):
        pcols_out[k] = band_table(lambda t: pc[t], PSF_TAPS, 128, 7 + 128 * (k - 1))
    for k in range(2):
        lag = iota((128, 128), 1) - iota((128, 128), 0) - 9 + 128 * k
        table = jnp.zeros((128, 128), F32)
        for t in range(PSF_TAPS):
            table = jnp.where(lag == t, pr[t], table)
        prows_out[k] = table.astype(BF16)
    lag = iota((128, LANES), 0) - (iota((128, LANES), 1) & 31)
    table = jnp.zeros((128, LANES), F32)
    for t in range(KTAPS):
        table = jnp.where(lag == t, kcl[t : t + 1, :], table)
    stamp_out[...] = table.astype(BF16)
    ready_out[...] = jnp.zeros(ready_out.shape, F32)
    for q in range(3):
        for g in range(4):
            lag = iota((32, 64), 1) - iota((32, 64), 0)
            table = jnp.zeros((32, 64), F32)
            for t in range(KTAPS):
                table = jnp.where(lag == t, kr[4 * q + g, t], table)
            down_out[q, 32 * g : 32 * g + 32] = table.astype(BF16)
    seam_out[...] = jnp.zeros(seam_out.shape, BF16)
    place = ((iota((32, 128), 1) + 16) & 31) - 16
    source = iota((32, 128), 0) - 16
    crosses = (place >= -10) & (place < 10) & ((place < 0) != (source < 0))
    lag = jnp.where(crosses, source - place + 10, -1)
    for v in range(3):
        taps = pltpu.roll(kcl[:, 128 * v : 128 * v + 128], 112, 1)
        table = jnp.zeros((32, 128), F32)
        for t in range(KTAPS):
            table = jnp.where(lag == t, taps[t : t + 1, :], table)
        seam_out[112:144, 128 * v : 128 * v + 128] = table.astype(BF16)

    own, ccds = lax.axis_index("ccd"), lax.axis_size("ccd")
    cap = slot_out.shape[0] * 2 // ccds

    def clear(v, c):
        count[v] = 0
        return c

    lax.fori_loop(0, ccds, clear, 0)

    def seat(m, c):
        v = shift[m]
        k = count[v]
        count[v] = k + 1
        slot_out[m] = lax.rem(own + v, ccds) * cap + k
        pick_out[m] = lax.rem(own - v + ccds, ccds) * cap + k
        return c

    lax.fori_loop(0, slot_out.shape[0], seat, 0)
    lane = iota((32, 128), 1)

    def cut(s, c):
        sky = jnp.where(lane < 32, window(science, srow[s], 32, scol[s]), 0.0)
        sky = sky + pltpu.roll(sky, 32, 1)
        sky_out[s] = sky + pltpu.roll(sky, 64, 1)
        return c

    lax.fori_loop(0, STAMPS, cut, 0)


def tables(kern_row, kern_col, psf_row, psf_col, band_shift, stamp_row, stamp_col, science):
    kc = kern_col.astype(F32)
    expand = lambda taps: jnp.pad(jnp.repeat(taps.T, 32, axis=1), ((0, 3), (0, 0)))
    return pl.pallas_call(
        tables_body,
        out_shape=(
            shape((BASIS, 3, 128, 128), BF16),
            shape((BASIS, STEP, SPAN), BF16),
            shape((3, 128, 128), BF16),
            shape((2, 128, 128), BF16),
            shape((128, LANES), BF16),
            shape((8, 128), F32),
            shape((3, 128, WIN), BF16),
            shape((256, LANES), BF16),
            shape(band_shift.shape, I32),
            shape(band_shift.shape, I32),
            shape((STAMPS, 32, 128), F32),
        ),
        in_specs=[smem()] * 4 + [vmem()] + [smem()] * 3 + [vmem()],
        out_specs=(vmem(),) * 8 + (smem(),) * 2 + (vmem(),),
        scratch_shapes=[pltpu.SMEM((64,), I32)],
        compiler_params=params(16),
        cost_estimate=cost(2 * 10**9, 4 * 10**6),
        name="tables",
    )(
        kern_row.astype(F32), kc, psf_row.astype(F32), psf_col.astype(F32),
        expand(kc),
        band_shift, stamp_row, stamp_col, science,
    )


def coadd_body(arrived, ready, out, edge, held):
    senders = arrived.shape[0]
    half = senders * 8
    told = arrived[:, 8].astype(F32).reshape(half, 128).T
    target = jnp.concatenate(
        [told[64 * k : 64 * k + 1] * 32.0 + told[64 * k + 32 : 64 * k + 33] for k in range(2)], axis=1
    ).astype(I32)
    for k in range(2):
        for q in range(4):
            part = arrived[:, 4 * k + q].astype(F32).reshape(half, 128)
            held[half * k : half * (k + 1), 128 * q : 128 * (q + 1)] = part.astype(BF16)
    for m in range(0, ROWS, 256):
        hit = (iota((256, 2 * half), 0) + m) == target
        placer = jnp.where(hit, 1.0, 0.0).astype(BF16)
        out[m : m + 256] = jnp.dot(placer, held[...], preferred_element_type=F32).astype(BF16)
    strip = lax.axis_index("strip")

    @pl.when(strip == 0)
    def _():
        edge[...] = out[ROWS - PAD :]

    @pl.when(strip != 0)
    def _():
        edge[...] = out[:PAD]


def coadd(arrived, ready):
    senders = arrived.shape[0]
    return pl.pallas_call(
        coadd_body,
        out_shape=(shape((ROWS, COLS), BF16), shape((PAD, COLS), BF16)),
        in_specs=[vmem(), vmem()],
        out_specs=(vmem(), vmem()),
        scratch_shapes=[pltpu.VMEM((senders * 16, COLS), BF16)],
        compiler_params=params(16),
        name="coadd",
    )(arrived, ready)


def frame(framed, image, near):
    strip = lax.axis_index("strip")
    rows = near[...].astype(F32)
    framed[PAD : PAD + ROWS] = image[...].astype(framed.dtype)
    framed[:PAD] = jnp.where(strip == 0, 0.0, rows).astype(framed.dtype)
    framed[PAD + ROWS :] = jnp.where(strip == 0, rows, 0.0).astype(framed.dtype)


def stamps_body(image, near, sigma, srow, scol, table, down, sky, out, framed, wins, across, basis):
    frame(framed, image, near)
    lane = iota((WIN, 128), 1)

    def cut(s, c):
        first = scol[s] - 10
        block = window(framed, srow[s] + 6, WIN, first)
        inside = (lane < 52) & (lane + first >= 0) & (lane + first < COLS)
        wins[s] = jnp.where(inside, block, 0.0).astype(BF16)
        return c

    lax.fori_loop(0, STAMPS, cut, 0, unroll=4)
    wide = jnp.dot(
        wins[...].reshape(STAMPS * WIN, 128), table[...], preferred_element_type=F32
    )
    across[...] = wide.astype(BF16).reshape(STAMPS, WIN, LANES)
    group = iota((32, 128), 1) >> 5

    def rows(s, total):
        parts = []
        for q in range(3):
            every = jnp.dot(
                down[q], across[s, :, 128 * q : 128 * q + 128], preferred_element_type=F32
            )
            acc = every[:32]
            for g in range(1, 4):
                acc = jnp.where(group == g, every[32 * g : 32 * g + 32], acc)
            done = acc.astype(BF16)
            basis[pl.ds(pl.multiple_of(s * 32, 32), 32), 128 * q : 128 * q + 128] = done
            parts.append(total[q] + jnp.sum(done.astype(F32) * sky[s], axis=0, keepdims=True))
        return tuple(parts)

    total = lax.fori_loop(
        0, STAMPS, rows, tuple(jnp.zeros((1, 128), F32) for _ in range(3)), unroll=4
    )
    total = jnp.concatenate(total, axis=1)
    pairs = lax.dot_general(
        basis[...], basis[...], (((0,), (0,)), ((), ())), preferred_element_type=F32
    )
    same = (iota((LANES, LANES), 0) & 31) == (iota((LANES, LANES), 1) & 31)
    pairs = jnp.where(same, pairs, 0.0)
    gram = [jnp.sum(pairs[32 * b : 32 * b + 32], axis=0, keepdims=True) for b in range(BASIS)]
    gram = jnp.concatenate(gram + [total, jnp.zeros((3, LANES), F32)], axis=0)
    parts = []
    for q in range(3):
        part = gram[:, 128 * q : 128 * q + 128]
        for turn in (1, 2, 4, 8, 16):
            part = part + pltpu.roll(part, 128 - turn, 1)
        parts.append(part)
    row, col = iota((16, 128), 0), iota((16, 128), 1)
    both = jnp.zeros((16, 128), F32)
    goal = jnp.zeros((16, 1), F32)
    for b in range(BASIS):
        entry = parts[b // 4][:, 32 * (b & 3) : 32 * (b & 3) + 1]
        both = jnp.where((col & 15) == b, entry, both)
        goal = jnp.where(row[:, :1] == b, entry[BASIS : BASIS + 1], goal)
    both = jnp.where((col & 15) == BASIS, goal, both)
    both = jnp.where(((col >> 4) == (row & 7)) & (row < BASIS), both, 0.0)
    both = both / (sigma[0] * sigma[0])
    packed = jnp.concatenate(
        [jnp.sum(both[:8], axis=0, keepdims=True), jnp.sum(both[8:], axis=0, keepdims=True)], axis=0
    )
    out[...] = jnp.broadcast_to(packed[None], out.shape)


def stamp_sums(image, near, sigma, srow, scol, table, down, sky, devices):
    return pl.pallas_call(
        stamps_body,
        out_shape=shape((devices, 2, 128), F32),
        in_specs=[vmem(), vmem(), smem(), smem(), smem(), vmem(), vmem(), vmem()],
        out_specs=vmem(),
        scratch_shapes=[
            pltpu.VMEM((FRAMED, COLS), F32),
            pltpu.VMEM((STAMPS, WIN, 128), BF16),
            pltpu.VMEM((STAMPS, WIN, LANES), BF16),
            pltpu.VMEM((STAMPS * 32, LANES), BF16),
        ],
        compiler_params=params(16),
        name="stamp_sums",
    )(image, near, sigma, srow, scol, table, down, sky)


def fill_cols(wide, blocks):
    for i in range(4):
        for o in range(4):
            if abs(i - o) <= 1:
                wide[128 * i : 128 * i + 128, 128 * o : 128 * o + 128] = blocks[i - o + 1]
            else:
                wide[128 * i : 128 * i + 128, 128 * o : 128 * o + 128] = jnp.zeros((128, 128), BF16)


def across_body(image, near, blocks, seam, out, framed, wide, border, held, sems):
    frame(framed, image, near)
    for m in range(0, FRAMED, 352):
        for v in range(3):
            border[v, m : m + 352] = jnp.dot(
                framed[m : m + 352, 128:384],
                seam[:, 128 * v : 128 * v + 128],
                preferred_element_type=F32,
            )
    lane = iota((352, 128), 1)

    def save(b, g):
        return pltpu.make_async_copy(held.at[g], out.at[b], sems.at[g])

    def four(v, c):
        for g in range(4):
            b = 4 * v + g
            for i in range(2):
                for o in range(2):
                    wide[128 * i : 128 * i + 128, 128 * o : 128 * o + 128] = blocks[b, i - o + 1]

            @pl.when(v > 0)
            def _():
                save(b - 4, g).wait()

            for m in range(0, FRAMED, 352):
                rows = slice(m, m + 352)
                left = jnp.dot(framed[rows, :256], wide[...], preferred_element_type=F32)
                right = jnp.dot(framed[rows, 256:], wide[...], preferred_element_type=F32)
                extra = border[v, rows]
                if g:
                    extra = pltpu.roll(extra, 128 - 32 * g, 1)
                held[g, rows, :128] = left[:, :128].astype(BF16)
                held[g, rows, 128:256] = (
                    left[:, 128:] + jnp.where(lane >= 118, extra, 0.0)
                ).astype(BF16)
                held[g, rows, 256:384] = (
                    right[:, :128] + jnp.where(lane < 10, extra, 0.0)
                ).astype(BF16)
                held[g, rows, 384:] = right[:, 128:].astype(BF16)
            save(b, g).start()
        return c

    lax.fori_loop(0, BASIS // 4, four, 0)
    for g in range(4):
        save(BASIS - 4 + g, g).wait()


def across_all(image, near, blocks, seam):
    return pl.pallas_call(
        across_body,
        out_shape=shape((BASIS, FRAMED, COLS), BF16),
        in_specs=[vmem()] * 4,
        out_specs=hbm(),
        scratch_shapes=[
            pltpu.VMEM((FRAMED, COLS), BF16),
            pltpu.VMEM((256, 256), BF16),
            pltpu.VMEM((3, FRAMED, 128), F32),
            pltpu.VMEM((4, FRAMED, COLS), BF16),
            pltpu.SemaphoreType.DMA((4,)),
        ],
        compiler_params=params(54),
        cost_estimate=cost(BASIS * FRAMED * COLS * COLS, 16 * 10**6),
        name="across",
    )(image, near, blocks, seam)


def solve(sums):
    total = jnp.sum(sums[...], axis=0)
    row, col = iota((16, 128), 0), iota((16, 128), 1)
    both = jnp.where(row < 8, total[0:1], total[1:2])
    both = jnp.where((col >> 4) == (row & 7), both, 0.0)
    for turn in (64, 32, 16):
        both = both + pltpu.roll(both, turn, 1)
    for k in range(BASIS):
        pivot = both[k : k + 1] / both[k : k + 1, k : k + 1]
        both = jnp.where(row == k, pivot, both - both[:, k : k + 1] * pivot)
    return both[:, BASIS : BASIS + 1]


def difference_body(
    across_in, sums_in, sigma_in, slot_in, table_in, science_in, coef_out, diff_out, leave_out,
    across, table, science, sums, sigma, slot, coef, bands, sems, load_sems, save_sems,
):
    ends = [0] + [first + span for first, _, span in BLOCKS]

    def load(i):
        some = pl.ds(ends[i], ends[i + 1] - ends[i])
        return pltpu.make_async_copy(
            across_in.at[:, some, :], across.at[:, some, :], load_sems.at[i]
        )

    small = [
        pltpu.make_async_copy(src, dst, sems.at[i])
        for i, (src, dst) in enumerate([(sums_in, sums), (sigma_in, sigma), (slot_in, slot)])
    ]
    table_load = pltpu.make_async_copy(table_in, table, sems.at[3])
    science_load = pltpu.make_async_copy(science_in, science, sems.at[4])
    for one in small:
        one.start()
    load(0).start()
    table_load.start()
    for one in small:
        one.wait()
    found = solve(sums)
    coef[...] = jnp.broadcast_to(found, coef.shape)
    eye = iota((16, 128), 0) == iota((16, 128), 1)
    coef_out[...] = jnp.sum(jnp.where(eye, found, 0.0), axis=0, keepdims=True)
    science_load.start()
    for i in range(1, len(BLOCKS)):
        load(i).start()
    scale = 1.0 / sigma[0]
    saves = []
    for i, (first, rows, span) in enumerate(BLOCKS):
        load(i).wait()
        if i == 0:
            table_load.wait()
        for h in range(0, COLS, 256):
            model = None
            for b in range(BASIS):
                basis = jnp.dot(
                    table[b, :rows, :span],
                    across[b, first : first + span, h : h + 256],
                    preferred_element_type=F32,
                )
                term = coef[b : b + 1, :] * basis.astype(BF16).astype(F32)
                model = term if model is None else model + term
            if i == 0 and h == 0:
                science_load.wait()
            left = (science[first : first + rows, h : h + 256] - model) * scale
            bands[first // 8 : (first + rows) // 8, :, h : h + 256] = left.reshape(
                rows // 8, 8, 256
            ).astype(BF16)

        def send(band, c):
            pltpu.make_async_copy(
                bands.at[band], leave_out.at[slot[band]], save_sems.at[0]
            ).start()
            return c

        lax.fori_loop(first // 8, (first + rows) // 8, send, 0, unroll=4)
        some = pl.ds(first // 8, rows // 8)
        saves.append(pltpu.make_async_copy(bands.at[some], diff_out.at[some], save_sems.at[1 + i]))
        saves[-1].start()
    for save in saves:
        save.wait()
    pltpu.make_async_copy(bands, leave_out.at[pl.ds(0, ROWS // 8)], save_sems.at[0]).wait()


def difference_all(sums, across, table, science, sigma, slot, slots):
    return pl.pallas_call(
        difference_body,
        out_shape=(
            shape((1, 128), F32),
            shape((ROWS // 8, 8, COLS), BF16),
            shape((slots, 8, COLS), BF16),
        ),
        in_specs=[hbm()] * 6,
        out_specs=(vmem(), hbm(), hbm()),
        scratch_shapes=[
            pltpu.VMEM((BASIS, FRAMED, COLS), BF16),
            pltpu.VMEM(table.shape, BF16),
            pltpu.VMEM(science.shape, F32),
            pltpu.VMEM(sums.shape, F32),
            pltpu.SMEM((1,), F32),
            pltpu.SMEM(slot.shape, I32),
            pltpu.VMEM((16, 256), F32),
            pltpu.VMEM((ROWS // 8, 8, COLS), BF16),
            pltpu.SemaphoreType.DMA((5,)),
            pltpu.SemaphoreType.DMA((len(BLOCKS),)),
            pltpu.SemaphoreType.DMA((1 + len(BLOCKS),)),
        ],
        compiler_params=params(53),
        name="difference",
    )(across, sums, sigma, slot, table, science)


def cut_body(diff, srow, scol, out, wide):
    wide[...] = diff[...].astype(F32).reshape(ROWS, COLS)
    row, lane = iota((32, 128), 0), iota((32, 128), 1)
    pick = (iota((8, 32), 1) >> 2 == iota((8, 32), 0)).astype(BF16)

    def cut(s, c):
        block = jnp.where(lane < 32, window(wide, srow[s], 32, scol[s]), 0.0)
        block = block + pltpu.roll(block, 32, 1)
        block = block + pltpu.roll(block, 64, 1)
        block = jnp.where((lane >> 5) == (row & 3), block, 0.0).astype(BF16)
        out[s] = jnp.dot(pick, block, preferred_element_type=F32).astype(BF16)
        return c

    lax.fori_loop(0, STAMPS, cut, 0)


def cut_stamps(diff, srow, scol):
    return pl.pallas_call(
        cut_body,
        out_shape=shape((STAMPS, 8, 128), BF16),
        in_specs=[vmem(), smem(), smem()],
        out_specs=vmem(),
        scratch_shapes=[pltpu.VMEM((ROWS, COLS), F32)],
        compiler_params=params(16),
        cost_estimate=cost(10**8, 3 * 10**6),
        name="cut_stamps",
    )(diff, srow, scol)


def smooth_body(landed, pick, blocks, out, patch, wide):
    fill_cols(wide, blocks)
    for first in range(0, ROWS, 256):

        def gather(m, c):
            pair = jnp.concatenate(
                [landed[pick[2 * m]].astype(F32), landed[pick[2 * m + 1]].astype(F32)], axis=0
            )
            patch[pl.ds(pl.multiple_of(m * 16, 16), 16)] = pair.astype(BF16)
            return c

        lax.fori_loop(first // 16, first // 16 + 16, gather, 0, unroll=4)
        out[first : first + 256] = jnp.dot(
            patch[first : first + 256], wide[...], preferred_element_type=F32
        ).astype(BF16)


def smooth(landed, pick, blocks):
    return pl.pallas_call(
        smooth_body,
        out_shape=shape((ROWS, COLS), BF16),
        in_specs=[vmem(), smem(), vmem()],
        out_specs=vmem(),
        scratch_shapes=[pltpu.VMEM((ROWS, COLS), BF16), pltpu.VMEM((COLS, COLS), BF16)],
        compiler_params=params(16),
        cost_estimate=cost(2 * ROWS * COLS * COLS, 3 * 10**6),
        name="smooth",
    )(landed, pick, blocks)


def fill_rows(table, blocks):
    table[:128, :128] = blocks[0]
    table[:128, 128:] = blocks[1]
    table[128:, :128] = jnp.zeros((STEP - 128, 128), BF16)
    table[128:, 128:] = blocks[0][: STEP - 128]


def filter_body(smoothed, near, cblocks, rblocks, out, framed, wide, table, tail, held, sems):
    fill_cols(wide, cblocks)
    fill_rows(table, rblocks)
    tail[...] = jnp.concatenate(
        [near[...].astype(F32), jnp.zeros((8, COLS), F32)], axis=0
    ).astype(BF16)
    edge = jnp.dot(tail[...], wide[...], preferred_element_type=F32)
    edge = jnp.where(lax.axis_index("strip") == 0, edge, jnp.concatenate([edge[8:], edge[:8]], axis=0))
    frame(framed, smoothed, edge.astype(BF16))
    saves = []
    for first, rows, span in BLOCKS:
        held[first : first + rows] = jnp.dot(
            table[:rows, :span], framed[first : first + span], preferred_element_type=F32
        )
        some = pl.ds(first, rows)
        saves.append(pltpu.make_async_copy(held.at[some], out.at[some], sems.at[len(saves)]))
        saves[-1].start()
    for save in saves:
        save.wait()


def filter_rows(smoothed, near, cblocks, rblocks):
    return pl.pallas_call(
        filter_body,
        out_shape=shape((ROWS, COLS), F32),
        in_specs=[vmem()] * 4,
        out_specs=hbm(),
        scratch_shapes=[
            pltpu.VMEM((FRAMED, COLS), BF16),
            pltpu.VMEM((COLS, COLS), BF16),
            pltpu.VMEM((STEP, SPAN), BF16),
            pltpu.VMEM((PAD, COLS), BF16),
            pltpu.VMEM((ROWS, COLS), F32),
            pltpu.SemaphoreType.DMA((len(BLOCKS),)),
        ],
        compiler_params=params(16),
        name="filter_rows",
    )(smoothed, near, cblocks, rblocks)


def shards(
    template, route_dest, route_row, kern_row, kern_col, science, noise_sigma,
    stamp_row, stamp_col, band_shift, psf_row, psf_col,
):
    ccds = lax.axis_size("ccd")
    devices = ccds * lax.axis_size("strip")
    bands = band_shift.shape[0]
    cap = 2 * bands // ccds
    outgoing = pack(route_dest, route_row, template, devices)
    arrived = lax.all_to_all(outgoing, BOTH, split_axis=0, concat_axis=0, tiled=True)
    cols, rows, pcols, prows, stamp_table, ready, down, seam, slot, pick, sky = tables(
        kern_row, kern_col, psf_row, psf_col, band_shift, stamp_row, stamp_col, science
    )
    image, edge = coadd(arrived, ready)
    near = lax.ppermute(edge, "strip", SWAP)
    sums = stamp_sums(
        image, near, noise_sigma, stamp_row, stamp_col, stamp_table, down, sky, devices
    )
    sums = lax.all_to_all(sums, BOTH, split_axis=0, concat_axis=0, tiled=True)
    across = across_all(image, near, cols, seam)
    coef, diff, leaving = difference_all(
        sums, across, rows, science, noise_sigma, slot, ccds * cap
    )
    landed = lax.all_to_all(
        leaving.reshape(ccds, cap, 8, COLS), "ccd", split_axis=0, concat_axis=0, tiled=True
    ).reshape(ccds * cap, 8, COLS)
    stamp_cut = cut_stamps(diff, stamp_row, stamp_col).reshape(STAMPS, 1024)
    last = jnp.where(lax.axis_index("strip") == 0, pick[bands - 1], pick[0])
    beside = lax.ppermute(
        lax.dynamic_slice(landed, (last, 0, 0), (1, 8, COLS))[0], "strip", SWAP
    )
    smoothed = smooth(landed, pick, pcols)
    filtered = filter_rows(smoothed, beside, pcols, prows)
    return (diff.reshape(ROWS, COLS), stamp_cut, coef[0, :BASIS], filtered)


def solution(mesh):
    placed = (
        P(BOTH, None, None), P(BOTH), P(BOTH), P(), P(), P(BOTH, None),
        P(BOTH), P(BOTH), P(BOTH), P(), P(), P(),
    )
    return jax.shard_map(
        shards,
        mesh=mesh,
        in_specs=placed,
        out_specs=(P(BOTH, None), P(BOTH, None), P(), P(BOTH, None)),
        check_vma=False,
    )
```

```python
import jax
import jax.numpy as jnp
from jax import lax
from jax.experimental import pallas as pl
from jax.experimental.pallas import tpu as pltpu
from jax.sharding import PartitionSpec as P

BASIS = 12
KTAPS = 21
PSF_TAPS = 15
STAMPS = 16
ROWS = 1024
COLS = 512
PAD = 16
FRAMED = ROWS + 2 * PAD
STEP = 224
SPAN = 256
WIN = 64
LANES = BASIS * 32
LARGE = 58
BOTH = ("ccd", "strip")
SWAP = [(0, 1), (1, 0)]
F32 = jnp.float32
BF16 = jnp.bfloat16
I32 = jnp.int32
HIGH = lax.Precision.HIGHEST

BLOCKS = [(j, min(STEP, ROWS - j), min(SPAN, FRAMED - j)) for j in range(0, ROWS, STEP)]


def vmem():
    return pl.BlockSpec(memory_space=pltpu.VMEM)


def hbm():
    return pl.BlockSpec(memory_space=pltpu.HBM)


def smem():
    return pl.BlockSpec(memory_space=pltpu.SMEM)


def params(mib):
    return pltpu.CompilerParams(vmem_limit_bytes=mib * 2**20)


def iota(shape, dim):
    return lax.broadcasted_iota(I32, shape, dim)


def shape(dims, dtype):
    return jax.ShapeDtypeStruct(dims, dtype)


def cost(flops, moved):
    return pl.CostEstimate(flops=flops, bytes_accessed=moved, transcendentals=0)


CHUNKS = 8


def pack_body(dest_in, row_in, pieces_in, sent, dest, row, pieces, out, count, rows, sems):
    devices = out.shape[0]
    loads = [
        pltpu.make_async_copy(src, dst, sems.at[CHUNKS + i])
        for i, (src, dst) in enumerate([(dest_in, dest), (row_in, row), (pieces_in, pieces)])
    ]
    for load in loads:
        load.start()
    out[...] = jnp.zeros(out.shape, out.dtype)

    def clear(d, c):
        count[d] = 0
        rows[2 * d] = 4096
        rows[2 * d + 1] = 4096
        return c

    lax.fori_loop(0, devices, clear, 0, unroll=8)
    for load in loads:
        load.wait()

    def place(i, c):
        d = dest[i]
        k = count[d]
        count[d] = k + 1
        rows[2 * d + k] = row[i]
        piece = pieces[i]
        for q in range(4):
            out[d, 4 * k + q] = piece[:, 128 * q : 128 * (q + 1)]
        return c

    lax.fori_loop(0, pieces.shape[0], place, 0, unroll=8)
    sub, lane = iota((8, 128), 0), iota((8, 128), 1)

    def tell(d, c):
        target = jnp.where(lane < 64, rows[2 * d], rows[2 * d + 1]) + sub
        told = jnp.where((lane & 32) == 0, target >> 5, target & 31)
        out[d, 8] = told.astype(F32).astype(BF16)
        return c

    part = devices // CHUNKS
    sends = []
    for i in range(CHUNKS):
        lax.fori_loop(i * part, (i + 1) * part, tell, 0, unroll=8)
        some = pl.ds(i * part, part)
        sends.append(pltpu.make_async_copy(out.at[some], sent.at[some], sems.at[i]))
        sends[-1].start()
    for send in sends:
        send.wait()


def pack(route_dest, route_row, template, devices):
    pieces = template.shape[0]
    return pl.pallas_call(
        pack_body,
        out_shape=shape((devices, 9, 8, 128), BF16),
        in_specs=[hbm()] * 3,
        out_specs=hbm(),
        scratch_shapes=[
            pltpu.SMEM((pieces,), I32),
            pltpu.SMEM((pieces,), I32),
            pltpu.VMEM(template.shape, BF16),
            pltpu.VMEM((devices, 9, 8, 128), BF16),
            pltpu.SMEM((devices,), I32),
            pltpu.SMEM((2 * devices,), I32),
            pltpu.SemaphoreType.DMA((CHUNKS + 3,)),
        ],
        compiler_params=params(LARGE),
        name="pack",
    )(route_dest, route_row, template)


def band_table(taps, count, size, offset):
    lag = iota((128, 128), 0) - iota((128, 128), 1) + offset
    table = jnp.zeros((128, 128), F32)
    for t in range(count):
        if -127 <= t - offset <= 127:
            table = jnp.where(lag == t, taps(t), table)
    return table.astype(BF16)


def window(ref, first_row, rows, first_col):
    tile = jnp.minimum(jnp.maximum(first_col, 0) >> 7, 2) * 128
    top = jnp.minimum((first_row >> 3) * 8, ref.shape[0] - rows - 8)
    block = ref[pl.ds(pl.multiple_of(top, 8), rows + 8), pl.ds(pl.multiple_of(tile, 128), 256)]
    turn = (256 - (first_col - tile)) & 255
    block = pltpu.roll(block, turn, 1)[:, :128]
    return pltpu.roll(block, lax.rem(rows + 8 - (first_row - top), rows + 8), 0)[:rows]


def tables_body(
    kr, kc, pr, pc, kcl, shift, srow, scol, science,
    cols_out, rows_out, pcols_out, prows_out, stamp_out, ready_out, down_out, seam_out,
    slot_out, pick_out, sky_out, count,
):
    for b in range(BASIS):
        for k in range(3):
            cols_out[b, k] = band_table(lambda t: kc[b, t], KTAPS, 128, 10 + 128 * (k - 1))
        for k in range(2):
            lag = iota((128, 128), 1) - iota((128, 128), 0) - 6 + 128 * k
            table = jnp.zeros((128, 128), F32)
            for t in range(KTAPS):
                table = jnp.where(lag == t, kr[b, t], table)
            table = table.astype(BF16)
            rows_out[b, :128, 128 * k : 128 * k + 128] = table
            if k == 0:
                rows_out[b, 128:, 128:] = table[: STEP - 128]
                rows_out[b, 128:, :128] = jnp.zeros((STEP - 128, 128), BF16)
    for k in range(3):
        pcols_out[k] = band_table(lambda t: pc[t], PSF_TAPS, 128, 7 + 128 * (k - 1))
    for k in range(2):
        lag = iota((128, 128), 1) - iota((128, 128), 0) - 9 + 128 * k
        table = jnp.zeros((128, 128), F32)
        for t in range(PSF_TAPS):
            table = jnp.where(lag == t, pr[t], table)
        prows_out[k] = table.astype(BF16)
    lag = iota((128, LANES), 0) - (iota((128, LANES), 1) & 31)
    table = jnp.zeros((128, LANES), F32)
    for t in range(KTAPS):
        table = jnp.where(lag == t, kcl[t : t + 1, :], table)
    stamp_out[...] = table.astype(BF16)
    ready_out[...] = jnp.zeros(ready_out.shape, F32)
    for q in range(3):
        for g in range(4):
            lag = iota((32, 64), 1) - iota((32, 64), 0)
            table = jnp.zeros((32, 64), F32)
            for t in range(KTAPS):
                table = jnp.where(lag == t, kr[4 * q + g, t], table)
            down_out[q, 32 * g : 32 * g + 32] = table.astype(BF16)
    seam_out[...] = jnp.zeros(seam_out.shape, BF16)
    place = ((iota((32, 128), 1) + 16) & 31) - 16
    source = iota((32, 128), 0) - 16
    crosses = (place >= -10) & (place < 10) & ((place < 0) != (source < 0))
    lag = jnp.where(crosses, source - place + 10, -1)
    for v in range(3):
        taps = pltpu.roll(kcl[:, 128 * v : 128 * v + 128], 112, 1)
        table = jnp.zeros((32, 128), F32)
        for t in range(KTAPS):
            table = jnp.where(lag == t, taps[t : t + 1, :], table)
        seam_out[112:144, 128 * v : 128 * v + 128] = table.astype(BF16)

    own, ccds = lax.axis_index("ccd"), lax.axis_size("ccd")
    cap = slot_out.shape[0] * 2 // ccds

    def clear(v, c):
        count[v] = 0
        return c

    lax.fori_loop(0, ccds, clear, 0)

    def seat(m, c):
        v = shift[m]
        k = count[v]
        count[v] = k + 1
        slot_out[m] = lax.rem(own + v, ccds) * cap + k
        pick_out[m] = lax.rem(own - v + ccds, ccds) * cap + k
        return c

    lax.fori_loop(0, slot_out.shape[0], seat, 0)
    lane = iota((32, 128), 1)

    def cut(s, c):
        sky = jnp.where(lane < 32, window(science, srow[s], 32, scol[s]), 0.0)
        sky = sky + pltpu.roll(sky, 32, 1)
        sky_out[s] = sky + pltpu.roll(sky, 64, 1)
        return c

    lax.fori_loop(0, STAMPS, cut, 0)


def tables(kern_row, kern_col, psf_row, psf_col, band_shift, stamp_row, stamp_col, science):
    kc = kern_col.astype(F32)
    expand = lambda taps: jnp.pad(jnp.repeat(taps.T, 32, axis=1), ((0, 3), (0, 0)))
    return pl.pallas_call(
        tables_body,
        out_shape=(
            shape((BASIS, 3, 128, 128), BF16),
            shape((BASIS, STEP, SPAN), BF16),
            shape((3, 128, 128), BF16),
            shape((2, 128, 128), BF16),
            shape((128, LANES), BF16),
            shape((8, 128), F32),
            shape((3, 128, WIN), BF16),
            shape((256, LANES), BF16),
            shape(band_shift.shape, I32),
            shape(band_shift.shape, I32),
            shape((STAMPS, 32, 128), F32),
        ),
        in_specs=[smem()] * 4 + [vmem()] + [smem()] * 3 + [vmem()],
        out_specs=(vmem(),) * 8 + (smem(),) * 2 + (vmem(),),
        scratch_shapes=[pltpu.SMEM((64,), I32)],
        compiler_params=params(16),
        cost_estimate=cost(2 * 10**9, 4 * 10**6),
        name="tables",
    )(
        kern_row.astype(F32), kc, psf_row.astype(F32), psf_col.astype(F32),
        expand(kc),
        band_shift, stamp_row, stamp_col, science,
    )


def coadd_body(arrived, ready, out, edge, held):
    senders = arrived.shape[0]
    half = senders * 8
    told = arrived[:, 8].astype(F32).reshape(half, 128).T
    target = jnp.concatenate(
        [told[64 * k : 64 * k + 1] * 32.0 + told[64 * k + 32 : 64 * k + 33] for k in range(2)], axis=1
    ).astype(I32)
    for k in range(2):
        for q in range(4):
            part = arrived[:, 4 * k + q].astype(F32).reshape(half, 128)
            held[half * k : half * (k + 1), 128 * q : 128 * (q + 1)] = part.astype(BF16)
    for m in range(0, ROWS, 256):
        hit = (iota((256, 2 * half), 0) + m) == target
        placer = jnp.where(hit, 1.0, 0.0).astype(BF16)
        out[m : m + 256] = jnp.dot(placer, held[...], preferred_element_type=F32).astype(BF16)
    strip = lax.axis_index("strip")

    @pl.when(strip == 0)
    def _():
        edge[...] = out[ROWS - PAD :]

    @pl.when(strip != 0)
    def _():
        edge[...] = out[:PAD]


def coadd(arrived, ready):
    senders = arrived.shape[0]
    return pl.pallas_call(
        coadd_body,
        out_shape=(shape((ROWS, COLS), BF16), shape((PAD, COLS), BF16)),
        in_specs=[vmem(), vmem()],
        out_specs=(vmem(), vmem()),
        scratch_shapes=[pltpu.VMEM((senders * 16, COLS), BF16)],
        compiler_params=params(16),
        name="coadd",
    )(arrived, ready)


def frame(framed, image, near):
    strip = lax.axis_index("strip")
    rows = near[...].astype(F32)
    framed[PAD : PAD + ROWS] = image[...].astype(framed.dtype)
    framed[:PAD] = jnp.where(strip == 0, 0.0, rows).astype(framed.dtype)
    framed[PAD + ROWS :] = jnp.where(strip == 0, rows, 0.0).astype(framed.dtype)


def stamps_body(image, near, sigma, srow, scol, table, down, sky, out, framed, wins, across, basis):
    frame(framed, image, near)
    lane = iota((WIN, 128), 1)

    def cut(s, c):
        first = scol[s] - 10
        block = window(framed, srow[s] + 6, WIN, first)
        inside = (lane < 52) & (lane + first >= 0) & (lane + first < COLS)
        wins[s] = jnp.where(inside, block, 0.0).astype(BF16)
        return c

    lax.fori_loop(0, STAMPS, cut, 0, unroll=4)
    wide = jnp.dot(
        wins[...].reshape(STAMPS * WIN, 128), table[...], preferred_element_type=F32
    )
    across[...] = wide.astype(BF16).reshape(STAMPS, WIN, LANES)
    group = iota((32, 128), 1) >> 5

    def rows(s, total):
        parts = []
        for q in range(3):
            every = jnp.dot(
                down[q], across[s, :, 128 * q : 128 * q + 128], preferred_element_type=F32
            )
            acc = every[:32]
            for g in range(1, 4):
                acc = jnp.where(group == g, every[32 * g : 32 * g + 32], acc)
            done = acc.astype(BF16)
            basis[pl.ds(pl.multiple_of(s * 32, 32), 32), 128 * q : 128 * q + 128] = done
            parts.append(total[q] + jnp.sum(done.astype(F32) * sky[s], axis=0, keepdims=True))
        return tuple(parts)

    total = lax.fori_loop(
        0, STAMPS, rows, tuple(jnp.zeros((1, 128), F32) for _ in range(3)), unroll=4
    )
    total = jnp.concatenate(total, axis=1)
    pairs = lax.dot_general(
        basis[...], basis[...], (((0,), (0,)), ((), ())), preferred_element_type=F32
    )
    same = (iota((LANES, LANES), 0) & 31) == (iota((LANES, LANES), 1) & 31)
    pairs = jnp.where(same, pairs, 0.0)
    gram = [jnp.sum(pairs[32 * b : 32 * b + 32], axis=0, keepdims=True) for b in range(BASIS)]
    gram = jnp.concatenate(gram + [total, jnp.zeros((3, LANES), F32)], axis=0)
    parts = []
    for q in range(3):
        part = gram[:, 128 * q : 128 * q + 128]
        for turn in (1, 2, 4, 8, 16):
            part = part + pltpu.roll(part, 128 - turn, 1)
        parts.append(part)
    row, col = iota((16, 128), 0), iota((16, 128), 1)
    both = jnp.zeros((16, 128), F32)
    goal = jnp.zeros((16, 1), F32)
    for b in range(BASIS):
        entry = parts[b // 4][:, 32 * (b & 3) : 32 * (b & 3) + 1]
        both = jnp.where((col & 15) == b, entry, both)
        goal = jnp.where(row[:, :1] == b, entry[BASIS : BASIS + 1], goal)
    both = jnp.where((col & 15) == BASIS, goal, both)
    both = jnp.where(((col >> 4) == (row & 7)) & (row < BASIS), both, 0.0)
    both = both / (sigma[0] * sigma[0])
    packed = jnp.concatenate(
        [jnp.sum(both[:8], axis=0, keepdims=True), jnp.sum(both[8:], axis=0, keepdims=True)], axis=0
    )
    out[...] = jnp.broadcast_to(packed[None], out.shape)


def stamp_sums(image, near, sigma, srow, scol, table, down, sky, devices):
    return pl.pallas_call(
        stamps_body,
        out_shape=shape((devices, 2, 128), F32),
        in_specs=[vmem(), vmem(), smem(), smem(), smem(), vmem(), vmem(), vmem()],
        out_specs=vmem(),
        scratch_shapes=[
            pltpu.VMEM((FRAMED, COLS), F32),
            pltpu.VMEM((STAMPS, WIN, 128), BF16),
            pltpu.VMEM((STAMPS, WIN, LANES), BF16),
            pltpu.VMEM((STAMPS * 32, LANES), BF16),
        ],
        compiler_params=params(16),
        name="stamp_sums",
    )(image, near, sigma, srow, scol, table, down, sky)


def fill_cols(wide, blocks):
    for i in range(4):
        for o in range(4):
            if abs(i - o) <= 1:
                wide[128 * i : 128 * i + 128, 128 * o : 128 * o + 128] = blocks[i - o + 1]
            else:
                wide[128 * i : 128 * i + 128, 128 * o : 128 * o + 128] = jnp.zeros((128, 128), BF16)


def across_body(image, near, blocks, seam, out, framed, wide, border, held, sems):
    frame(framed, image, near)
    for m in range(0, FRAMED, 352):
        for v in range(3):
            border[v, m : m + 352] = jnp.dot(
                framed[m : m + 352, 128:384],
                seam[:, 128 * v : 128 * v + 128],
                preferred_element_type=F32,
            )
    lane = iota((352, 128), 1)

    def save(b, g):
        return pltpu.make_async_copy(held.at[g], out.at[b], sems.at[g])

    def four(v, c):
        for g in range(4):
            b = 4 * v + g
            for i in range(2):
                for o in range(2):
                    wide[128 * i : 128 * i + 128, 128 * o : 128 * o + 128] = blocks[b, i - o + 1]

            @pl.when(v > 0)
            def _():
                save(b - 4, g).wait()

            for m in range(0, FRAMED, 352):
                rows = slice(m, m + 352)
                left = jnp.dot(framed[rows, :256], wide[...], preferred_element_type=F32)
                right = jnp.dot(framed[rows, 256:], wide[...], preferred_element_type=F32)
                extra = border[v, rows]
                if g:
                    extra = pltpu.roll(extra, 128 - 32 * g, 1)
                held[g, rows, :128] = left[:, :128].astype(BF16)
                held[g, rows, 128:256] = (
                    left[:, 128:] + jnp.where(lane >= 118, extra, 0.0)
                ).astype(BF16)
                held[g, rows, 256:384] = (
                    right[:, :128] + jnp.where(lane < 10, extra, 0.0)
                ).astype(BF16)
                held[g, rows, 384:] = right[:, 128:].astype(BF16)
            save(b, g).start()
        return c

    lax.fori_loop(0, BASIS // 4, four, 0)
    for g in range(4):
        save(BASIS - 4 + g, g).wait()


def across_all(image, near, blocks, seam):
    return pl.pallas_call(
        across_body,
        out_shape=shape((BASIS, FRAMED, COLS), BF16),
        in_specs=[vmem()] * 4,
        out_specs=hbm(),
        scratch_shapes=[
            pltpu.VMEM((FRAMED, COLS), BF16),
            pltpu.VMEM((256, 256), BF16),
            pltpu.VMEM((3, FRAMED, 128), F32),
            pltpu.VMEM((4, FRAMED, COLS), BF16),
            pltpu.SemaphoreType.DMA((4,)),
        ],
        compiler_params=params(50),
        cost_estimate=cost(BASIS * FRAMED * COLS * COLS, 16 * 10**6),
        name="across",
    )(image, near, blocks, seam)


def solve(sums):
    total = jnp.sum(sums[...], axis=0)
    row, col = iota((16, 128), 0), iota((16, 128), 1)
    both = jnp.where(row < 8, total[0:1], total[1:2])
    both = jnp.where((col >> 4) == (row & 7), both, 0.0)
    for turn in (64, 32, 16):
        both = both + pltpu.roll(both, turn, 1)
    for k in range(BASIS):
        pivot = both[k : k + 1] / both[k : k + 1, k : k + 1]
        both = jnp.where(row == k, pivot, both - both[:, k : k + 1] * pivot)
    return both[:, BASIS : BASIS + 1]


def difference_body(
    across_in, sums_in, sigma_in, slot_in, table_in, science_in, coef_out, diff_out, leave_out,
    across, table, science, sums, sigma, slot, coef, bands, sems, load_sems, sky_sems, save_sems,
):
    ends = [0] + [first + span for first, _, span in BLOCKS]

    def load(i):
        some = pl.ds(ends[i], ends[i + 1] - ends[i])
        return pltpu.make_async_copy(
            across_in.at[:, some, :], across.at[:, some, :], load_sems.at[i]
        )

    small = [
        pltpu.make_async_copy(src, dst, sems.at[i])
        for i, (src, dst) in enumerate([(sums_in, sums), (sigma_in, sigma), (slot_in, slot)])
    ]
    table_load = pltpu.make_async_copy(table_in, table, sems.at[3])

    def sky_load(i):
        some = pl.ds(BLOCKS[i][0], BLOCKS[i][1])
        return pltpu.make_async_copy(science_in.at[some], science.at[some], sky_sems.at[i])

    def ahead(i):
        if i < len(BLOCKS):
            load(i).start()
            sky_load(i).start()

    for one in small:
        one.start()
    load(0).start()
    table_load.start()
    for one in small:
        one.wait()
    found = solve(sums)
    coef[...] = jnp.broadcast_to(found, coef.shape)
    eye = iota((16, 128), 0) == iota((16, 128), 1)
    coef_out[...] = jnp.sum(jnp.where(eye, found, 0.0), axis=0, keepdims=True)
    sky_load(0).start()
    for i in range(1, 2):
        ahead(i)
    scale = 1.0 / sigma[0]
    saves = []
    for i, (first, rows, span) in enumerate(BLOCKS):
        load(i).wait()
        ahead(i + 2)
        if i == 0:
            table_load.wait()
        for h in range(0, COLS, 256):
            model = None
            for b in range(BASIS):
                basis = jnp.dot(
                    table[b, :rows, :span],
                    across[b, first : first + span, h : h + 256],
                    preferred_element_type=F32,
                )
                term = coef[b : b + 1, :] * basis.astype(BF16).astype(F32)
                model = term if model is None else model + term
            if h == 0:
                sky_load(i).wait()
            left = (science[first : first + rows, h : h + 256] - model) * scale
            bands[first // 8 : (first + rows) // 8, :, h : h + 256] = left.reshape(
                rows // 8, 8, 256
            ).astype(BF16)

        def send(band, c):
            pltpu.make_async_copy(
                bands.at[band], leave_out.at[slot[band]], save_sems.at[0]
            ).start()
            return c

        lax.fori_loop(first // 8, (first + rows) // 8, send, 0, unroll=4)
        some = pl.ds(first // 8, rows // 8)
        saves.append(pltpu.make_async_copy(bands.at[some], diff_out.at[some], save_sems.at[1 + i]))
        saves[-1].start()
    for save in saves:
        save.wait()
    pltpu.make_async_copy(bands, leave_out.at[pl.ds(0, ROWS // 8)], save_sems.at[0]).wait()


def difference_all(sums, across, table, science, sigma, slot, slots):
    return pl.pallas_call(
        difference_body,
        out_shape=(
            shape((1, 128), F32),
            shape((ROWS // 8, 8, COLS), BF16),
            shape((slots, 8, COLS), BF16),
        ),
        in_specs=[hbm()] * 6,
        out_specs=(vmem(), hbm(), hbm()),
        scratch_shapes=[
            pltpu.VMEM((BASIS, FRAMED, COLS), BF16),
            pltpu.VMEM(table.shape, BF16),
            pltpu.VMEM(science.shape, F32),
            pltpu.VMEM(sums.shape, F32),
            pltpu.SMEM((1,), F32),
            pltpu.SMEM(slot.shape, I32),
            pltpu.VMEM((16, 256), F32),
            pltpu.VMEM((ROWS // 8, 8, COLS), BF16),
            pltpu.SemaphoreType.DMA((4,)),
            pltpu.SemaphoreType.DMA((len(BLOCKS),)),
            pltpu.SemaphoreType.DMA((len(BLOCKS),)),
            pltpu.SemaphoreType.DMA((1 + len(BLOCKS),)),
        ],
        compiler_params=params(53),
        name="difference",
    )(across, sums, sigma, slot, table, science)


def cut_body(diff, srow, scol, out, wide):
    wide[...] = diff[...].astype(F32).reshape(ROWS, COLS)
    row, lane = iota((32, 128), 0), iota((32, 128), 1)
    pick = (iota((8, 32), 1) >> 2 == iota((8, 32), 0)).astype(BF16)

    def cut(s, c):
        block = jnp.where(lane < 32, window(wide, srow[s], 32, scol[s]), 0.0)
        block = block + pltpu.roll(block, 32, 1)
        block = block + pltpu.roll(block, 64, 1)
        block = jnp.where((lane >> 5) == (row & 3), block, 0.0).astype(BF16)
        out[s] = jnp.dot(pick, block, preferred_element_type=F32).astype(BF16)
        return c

    lax.fori_loop(0, STAMPS, cut, 0)


def cut_stamps(diff, srow, scol):
    return pl.pallas_call(
        cut_body,
        out_shape=shape((STAMPS, 8, 128), BF16),
        in_specs=[vmem(), smem(), smem()],
        out_specs=vmem(),
        scratch_shapes=[pltpu.VMEM((ROWS, COLS), F32)],
        compiler_params=params(16),
        cost_estimate=cost(10**8, 3 * 10**6),
        name="cut_stamps",
    )(diff, srow, scol)


def smooth_body(landed, pick, blocks, out, patch, wide):
    fill_cols(wide, blocks)
    for first in range(0, ROWS, 256):

        def gather(m, c):
            pair = jnp.concatenate(
                [landed[pick[2 * m]].astype(F32), landed[pick[2 * m + 1]].astype(F32)], axis=0
            )
            patch[pl.ds(pl.multiple_of(m * 16, 16), 16)] = pair.astype(BF16)
            return c

        lax.fori_loop(first // 16, first // 16 + 16, gather, 0, unroll=4)
        out[first : first + 256] = jnp.dot(
            patch[first : first + 256], wide[...], preferred_element_type=F32
        ).astype(BF16)


def smooth(landed, pick, blocks):
    return pl.pallas_call(
        smooth_body,
        out_shape=shape((ROWS, COLS), BF16),
        in_specs=[vmem(), smem(), vmem()],
        out_specs=vmem(),
        scratch_shapes=[pltpu.VMEM((ROWS, COLS), BF16), pltpu.VMEM((COLS, COLS), BF16)],
        compiler_params=params(16),
        cost_estimate=cost(2 * ROWS * COLS * COLS, 3 * 10**6),
        name="smooth",
    )(landed, pick, blocks)


def fill_rows(table, blocks):
    table[:128, :128] = blocks[0]
    table[:128, 128:] = blocks[1]
    table[128:, :128] = jnp.zeros((STEP - 128, 128), BF16)
    table[128:, 128:] = blocks[0][: STEP - 128]


def filter_body(smoothed, near, cblocks, rblocks, out, framed, wide, table, tail, held, sems):
    fill_cols(wide, cblocks)
    fill_rows(table, rblocks)
    tail[...] = jnp.concatenate(
        [near[...].astype(F32), jnp.zeros((8, COLS), F32)], axis=0
    ).astype(BF16)
    edge = jnp.dot(tail[...], wide[...], preferred_element_type=F32)
    edge = jnp.where(lax.axis_index("strip") == 0, edge, jnp.concatenate([edge[8:], edge[:8]], axis=0))
    frame(framed, smoothed, edge.astype(BF16))
    saves = []
    for first, rows, span in BLOCKS:
        held[first : first + rows] = jnp.dot(
            table[:rows, :span], framed[first : first + span], preferred_element_type=F32
        )
        some = pl.ds(first, rows)
        saves.append(pltpu.make_async_copy(held.at[some], out.at[some], sems.at[len(saves)]))
        saves[-1].start()
    for save in saves:
        save.wait()


def filter_rows(smoothed, near, cblocks, rblocks):
    return pl.pallas_call(
        filter_body,
        out_shape=shape((ROWS, COLS), F32),
        in_specs=[vmem()] * 4,
        out_specs=hbm(),
        scratch_shapes=[
            pltpu.VMEM((FRAMED, COLS), BF16),
            pltpu.VMEM((COLS, COLS), BF16),
            pltpu.VMEM((STEP, SPAN), BF16),
            pltpu.VMEM((PAD, COLS), BF16),
            pltpu.VMEM((ROWS, COLS), F32),
            pltpu.SemaphoreType.DMA((len(BLOCKS),)),
        ],
        compiler_params=params(16),
        name="filter_rows",
    )(smoothed, near, cblocks, rblocks)


def shards(
    template, route_dest, route_row, kern_row, kern_col, science, noise_sigma,
    stamp_row, stamp_col, band_shift, psf_row, psf_col,
):
    ccds = lax.axis_size("ccd")
    devices = ccds * lax.axis_size("strip")
    bands = band_shift.shape[0]
    cap = 2 * bands // ccds
    outgoing = pack(route_dest, route_row, template, devices)
    arrived = lax.all_to_all(outgoing, BOTH, split_axis=0, concat_axis=0, tiled=True)
    cols, rows, pcols, prows, stamp_table, ready, down, seam, slot, pick, sky = tables(
        kern_row, kern_col, psf_row, psf_col, band_shift, stamp_row, stamp_col, science
    )
    image, edge = coadd(arrived, ready)
    near = lax.ppermute(edge, "strip", SWAP)
    sums = stamp_sums(
        image, near, noise_sigma, stamp_row, stamp_col, stamp_table, down, sky, devices
    )
    sums = lax.all_to_all(sums, BOTH, split_axis=0, concat_axis=0, tiled=True)
    across = across_all(image, near, cols, seam)
    coef, diff, leaving = difference_all(
        sums, across, rows, science, noise_sigma, slot, ccds * cap
    )
    landed = lax.all_to_all(
        leaving.reshape(ccds, cap, 8, COLS), "ccd", split_axis=0, concat_axis=0, tiled=True
    ).reshape(ccds * cap, 8, COLS)
    stamp_cut = cut_stamps(diff, stamp_row, stamp_col).reshape(STAMPS, 1024)
    last = jnp.where(lax.axis_index("strip") == 0, pick[bands - 1], pick[0])
    beside = lax.ppermute(
        lax.dynamic_slice(landed, (last, 0, 0), (1, 8, COLS))[0], "strip", SWAP
    )
    smoothed = smooth(landed, pick, pcols)
    filtered = filter_rows(smoothed, beside, pcols, prows)
    return (diff.reshape(ROWS, COLS), stamp_cut, coef[0, :BASIS], filtered)


def solution(mesh):
    placed = (
        P(BOTH, None, None), P(BOTH), P(BOTH), P(), P(), P(BOTH, None),
        P(BOTH), P(BOTH), P(BOTH), P(), P(), P(),
    )
    return jax.shard_map(
        shards,
        mesh=mesh,
        in_specs=placed,
        out_specs=(P(BOTH, None), P(BOTH, None), P(), P(BOTH, None)),
        check_vma=False,
    )
```

```python
import jax
import jax.numpy as jnp
from jax import lax
from jax.experimental import pallas as pl
from jax.experimental.pallas import tpu as pltpu
from jax.sharding import PartitionSpec as P

BASIS = 12
KTAPS = 21
PSF_TAPS = 15
STAMPS = 16
ROWS = 1024
COLS = 512
PAD = 16
FRAMED = ROWS + 2 * PAD
STEP = 224
SPAN = 256
WIN = 64
LANES = BASIS * 32
LARGE = 58
BOTH = ("ccd", "strip")
SWAP = [(0, 1), (1, 0)]
F32 = jnp.float32
BF16 = jnp.bfloat16
I32 = jnp.int32
HIGH = lax.Precision.HIGHEST

BLOCKS = [(j, min(STEP, ROWS - j), min(SPAN, FRAMED - j)) for j in range(0, ROWS, STEP)]


def vmem():
    return pl.BlockSpec(memory_space=pltpu.VMEM)


def hbm():
    return pl.BlockSpec(memory_space=pltpu.HBM)


def smem():
    return pl.BlockSpec(memory_space=pltpu.SMEM)


def params(mib):
    return pltpu.CompilerParams(vmem_limit_bytes=mib * 2**20)


def iota(shape, dim):
    return lax.broadcasted_iota(I32, shape, dim)


def shape(dims, dtype):
    return jax.ShapeDtypeStruct(dims, dtype)


def cost(flops, moved):
    return pl.CostEstimate(flops=flops, bytes_accessed=moved, transcendentals=0)


CHUNKS = 8


def pack_body(dest_in, row_in, pieces_in, sent, dest, row, pieces, out, count, rows, sems):
    devices = out.shape[0]
    loads = [
        pltpu.make_async_copy(src, dst, sems.at[CHUNKS + i])
        for i, (src, dst) in enumerate([(dest_in, dest), (row_in, row), (pieces_in, pieces)])
    ]
    for load in loads:
        load.start()
    out[...] = jnp.zeros(out.shape, out.dtype)

    def clear(d, c):
        count[d] = 0
        rows[2 * d] = 4096
        rows[2 * d + 1] = 4096
        return c

    lax.fori_loop(0, devices, clear, 0, unroll=8)
    for load in loads:
        load.wait()

    def place(i, c):
        d = dest[i]
        k = count[d]
        count[d] = k + 1
        rows[2 * d + k] = row[i]
        piece = pieces[i]
        for q in range(4):
            out[d, 4 * k + q] = piece[:, 128 * q : 128 * (q + 1)]
        return c

    lax.fori_loop(0, pieces.shape[0], place, 0, unroll=8)
    sub, lane = iota((8, 128), 0), iota((8, 128), 1)

    def tell(d, c):
        target = jnp.where(lane < 64, rows[2 * d], rows[2 * d + 1]) + sub
        told = jnp.where((lane & 32) == 0, target >> 5, target & 31)
        out[d, 8] = told.astype(F32).astype(BF16)
        return c

    part = devices // CHUNKS
    sends = []
    for i in range(CHUNKS):
        lax.fori_loop(i * part, (i + 1) * part, tell, 0, unroll=8)
        some = pl.ds(i * part, part)
        sends.append(pltpu.make_async_copy(out.at[some], sent.at[some], sems.at[i]))
        sends[-1].start()
    for send in sends:
        send.wait()


def pack(route_dest, route_row, template, devices):
    pieces = template.shape[0]
    return pl.pallas_call(
        pack_body,
        out_shape=shape((devices, 9, 8, 128), BF16),
        in_specs=[hbm()] * 3,
        out_specs=hbm(),
        scratch_shapes=[
            pltpu.SMEM((pieces,), I32),
            pltpu.SMEM((pieces,), I32),
            pltpu.VMEM(template.shape, BF16),
            pltpu.VMEM((devices, 9, 8, 128), BF16),
            pltpu.SMEM((devices,), I32),
            pltpu.SMEM((2 * devices,), I32),
            pltpu.SemaphoreType.DMA((CHUNKS + 3,)),
        ],
        compiler_params=params(LARGE),
        name="pack",
    )(route_dest, route_row, template)


def band_table(taps, count, size, offset):
    lag = iota((128, 128), 0) - iota((128, 128), 1) + offset
    table = jnp.zeros((128, 128), F32)
    for t in range(count):
        if -127 <= t - offset <= 127:
            table = jnp.where(lag == t, taps(t), table)
    return table.astype(BF16)


def window(ref, first_row, rows, first_col):
    tile = jnp.minimum(jnp.maximum(first_col, 0) >> 7, 2) * 128
    top = jnp.minimum((first_row >> 3) * 8, ref.shape[0] - rows - 8)
    block = ref[pl.ds(pl.multiple_of(top, 8), rows + 8), pl.ds(pl.multiple_of(tile, 128), 256)]
    turn = (256 - (first_col - tile)) & 255
    block = pltpu.roll(block, turn, 1)[:, :128]
    return pltpu.roll(block, lax.rem(rows + 8 - (first_row - top), rows + 8), 0)[:rows]


def tables_body(
    kr, kc, pr, pc, kcl, shift, srow, scol, science,
    cols_out, rows_out, pcols_out, prows_out, stamp_out, ready_out, down_out,
    slot_out, pick_out, sky_out, count,
):
    for b in range(BASIS):
        for k in range(3):
            cols_out[b, k] = band_table(lambda t: kc[b, t], KTAPS, 128, 10 + 128 * (k - 1))
        for k in range(2):
            lag = iota((128, 128), 1) - iota((128, 128), 0) - 6 + 128 * k
            table = jnp.zeros((128, 128), F32)
            for t in range(KTAPS):
                table = jnp.where(lag == t, kr[b, t], table)
            table = table.astype(BF16)
            rows_out[b, :128, 128 * k : 128 * k + 128] = table
            if k == 0:
                rows_out[b, 128:, 128:] = table[: STEP - 128]
                rows_out[b, 128:, :128] = jnp.zeros((STEP - 128, 128), BF16)
    for k in range(3):
        pcols_out[k] = band_table(lambda t: pc[t], PSF_TAPS, 128, 7 + 128 * (k - 1))
    for k in range(2):
        lag = iota((128, 128), 1) - iota((128, 128), 0) - 9 + 128 * k
        table = jnp.zeros((128, 128), F32)
        for t in range(PSF_TAPS):
            table = jnp.where(lag == t, pr[t], table)
        prows_out[k] = table.astype(BF16)
    lag = iota((128, LANES), 0) - (iota((128, LANES), 1) & 31)
    table = jnp.zeros((128, LANES), F32)
    for t in range(KTAPS):
        table = jnp.where(lag == t, kcl[t : t + 1, :], table)
    stamp_out[...] = table.astype(BF16)
    ready_out[...] = jnp.zeros(ready_out.shape, F32)
    for q in range(3):
        for g in range(4):
            lag = iota((32, 64), 1) - iota((32, 64), 0)
            table = jnp.zeros((32, 64), F32)
            for t in range(KTAPS):
                table = jnp.where(lag == t, kr[4 * q + g, t], table)
            down_out[q, 32 * g : 32 * g + 32] = table.astype(BF16)
    nothing = jnp.zeros((112, 128), F32)
    place = ((iota((32, 128), 1) + 16) & 31) - 16
    source = iota((32, 128), 0) - 16
    crosses = (place >= -10) & (place < 10) & ((place < 0) != (source < 0))
    lag = jnp.where(crosses, source - place + 10, -1)
    for v in range(3):
        taps = pltpu.roll(kcl[:, 128 * v : 128 * v + 128], 112, 1)
        table = jnp.zeros((32, 128), F32)
        for t in range(KTAPS):
            table = jnp.where(lag == t, taps[t : t + 1, :], table)
        cols_out[BASIS, v] = jnp.concatenate([nothing, table[:16]], axis=0).astype(BF16)
        cols_out[BASIS + 1, v] = jnp.concatenate([table[16:], nothing], axis=0).astype(BF16)

    own, ccds = lax.axis_index("ccd"), lax.axis_size("ccd")
    cap = slot_out.shape[0] * 2 // ccds

    def clear(v, c):
        count[v] = 0
        return c

    lax.fori_loop(0, ccds, clear, 0)

    def seat(m, c):
        v = shift[m]
        k = count[v]
        count[v] = k + 1
        slot_out[m] = lax.rem(own + v, ccds) * cap + k
        pick_out[m] = lax.rem(own - v + ccds, ccds) * cap + k
        return c

    lax.fori_loop(0, slot_out.shape[0], seat, 0)
    lane = iota((32, 128), 1)

    def cut(s, c):
        sky = jnp.where(lane < 32, window(science, srow[s], 32, scol[s]), 0.0)
        sky = sky + pltpu.roll(sky, 32, 1)
        sky_out[s] = sky + pltpu.roll(sky, 64, 1)
        return c

    lax.fori_loop(0, STAMPS, cut, 0)


def tables(kern_row, kern_col, psf_row, psf_col, band_shift, stamp_row, stamp_col, science):
    kc = kern_col.astype(F32)
    expand = lambda taps: jnp.pad(jnp.repeat(taps.T, 32, axis=1), ((0, 3), (0, 0)))
    return pl.pallas_call(
        tables_body,
        out_shape=(
            shape((BASIS + 2, 3, 128, 128), BF16),
            shape((BASIS, STEP, SPAN), BF16),
            shape((3, 128, 128), BF16),
            shape((2, 128, 128), BF16),
            shape((128, LANES), BF16),
            shape((8, 128), F32),
            shape((3, 128, WIN), BF16),
            shape(band_shift.shape, I32),
            shape(band_shift.shape, I32),
            shape((STAMPS, 32, 128), F32),
        ),
        in_specs=[smem()] * 4 + [vmem()] + [smem()] * 3 + [vmem()],
        out_specs=(vmem(),) * 7 + (smem(),) * 2 + (vmem(),),
        scratch_shapes=[pltpu.SMEM((64,), I32)],
        compiler_params=params(16),
        cost_estimate=cost(2 * 10**9, 4 * 10**6),
        name="tables",
    )(
        kern_row.astype(F32), kc, psf_row.astype(F32), psf_col.astype(F32),
        expand(kc),
        band_shift, stamp_row, stamp_col, science,
    )


def coadd_body(arrived, ready, out, edge, held):
    senders = arrived.shape[0]
    half = senders * 8
    told = arrived[:, 8].astype(F32).reshape(half, 128).T
    target = jnp.concatenate(
        [told[64 * k : 64 * k + 1] * 32.0 + told[64 * k + 32 : 64 * k + 33] for k in range(2)], axis=1
    ).astype(I32)
    for k in range(2):
        for q in range(4):
            part = arrived[:, 4 * k + q].astype(F32).reshape(half, 128)
            held[half * k : half * (k + 1), 128 * q : 128 * (q + 1)] = part.astype(BF16)
    for m in range(0, ROWS, 256):
        hit = (iota((256, 2 * half), 0) + m) == target
        placer = jnp.where(hit, 1.0, 0.0).astype(BF16)
        out[m : m + 256] = jnp.dot(placer, held[...], preferred_element_type=F32).astype(BF16)
    strip = lax.axis_index("strip")

    @pl.when(strip == 0)
    def _():
        edge[...] = out[ROWS - PAD :]

    @pl.when(strip != 0)
    def _():
        edge[...] = out[:PAD]


def coadd(arrived, ready):
    senders = arrived.shape[0]
    return pl.pallas_call(
        coadd_body,
        out_shape=(shape((ROWS, COLS), BF16), shape((PAD, COLS), BF16)),
        in_specs=[vmem(), vmem()],
        out_specs=(vmem(), vmem()),
        scratch_shapes=[pltpu.VMEM((senders * 16, COLS), BF16)],
        compiler_params=params(16),
        name="coadd",
    )(arrived, ready)


def frame(framed, image, near):
    strip = lax.axis_index("strip")
    rows = near[...].astype(F32)
    framed[PAD : PAD + ROWS] = image[...].astype(framed.dtype)
    framed[:PAD] = jnp.where(strip == 0, 0.0, rows).astype(framed.dtype)
    framed[PAD + ROWS :] = jnp.where(strip == 0, rows, 0.0).astype(framed.dtype)


def stamps_body(image, near, sigma, srow, scol, table, down, sky, out, framed, wins, across, basis):
    frame(framed, image, near)
    lane = iota((WIN, 128), 1)

    def cut(s, c):
        first = scol[s] - 10
        block = window(framed, srow[s] + 6, WIN, first)
        inside = (lane < 52) & (lane + first >= 0) & (lane + first < COLS)
        wins[s] = jnp.where(inside, block, 0.0).astype(BF16)
        return c

    lax.fori_loop(0, STAMPS, cut, 0, unroll=4)
    wide = jnp.dot(
        wins[...].reshape(STAMPS * WIN, 128), table[...], preferred_element_type=F32
    )
    across[...] = wide.astype(BF16).reshape(STAMPS, WIN, LANES)
    group = iota((32, 128), 1) >> 5

    def rows(s, total):
        parts = []
        for q in range(3):
            every = jnp.dot(
                down[q], across[s, :, 128 * q : 128 * q + 128], preferred_element_type=F32
            )
            acc = every[:32]
            for g in range(1, 4):
                acc = jnp.where(group == g, every[32 * g : 32 * g + 32], acc)
            done = acc.astype(BF16)
            basis[pl.ds(pl.multiple_of(s * 32, 32), 32), 128 * q : 128 * q + 128] = done
            parts.append(total[q] + jnp.sum(done.astype(F32) * sky[s], axis=0, keepdims=True))
        return tuple(parts)

    total = lax.fori_loop(
        0, STAMPS, rows, tuple(jnp.zeros((1, 128), F32) for _ in range(3)), unroll=4
    )
    total = jnp.concatenate(total, axis=1)
    pairs = lax.dot_general(
        basis[...], basis[...], (((0,), (0,)), ((), ())), preferred_element_type=F32
    )
    same = (iota((LANES, LANES), 0) & 31) == (iota((LANES, LANES), 1) & 31)
    pairs = jnp.where(same, pairs, 0.0)
    gram = [jnp.sum(pairs[32 * b : 32 * b + 32], axis=0, keepdims=True) for b in range(BASIS)]
    gram = jnp.concatenate(gram + [total, jnp.zeros((3, LANES), F32)], axis=0)
    parts = []
    for q in range(3):
        part = gram[:, 128 * q : 128 * q + 128]
        for turn in (1, 2, 4, 8, 16):
            part = part + pltpu.roll(part, 128 - turn, 1)
        parts.append(part)
    row, col = iota((16, 128), 0), iota((16, 128), 1)
    both = jnp.zeros((16, 128), F32)
    goal = jnp.zeros((16, 1), F32)
    for b in range(BASIS):
        entry = parts[b // 4][:, 32 * (b & 3) : 32 * (b & 3) + 1]
        both = jnp.where((col & 15) == b, entry, both)
        goal = jnp.where(row[:, :1] == b, entry[BASIS : BASIS + 1], goal)
    both = jnp.where((col & 15) == BASIS, goal, both)
    both = jnp.where(((col >> 4) == (row & 7)) & (row < BASIS), both, 0.0)
    both = both / (sigma[0] * sigma[0])
    packed = jnp.concatenate(
        [jnp.sum(both[:8], axis=0, keepdims=True), jnp.sum(both[8:], axis=0, keepdims=True)], axis=0
    )
    out[...] = jnp.broadcast_to(packed[None], out.shape)


def stamp_sums(image, near, sigma, srow, scol, table, down, sky, devices):
    return pl.pallas_call(
        stamps_body,
        out_shape=shape((devices, 2, 128), F32),
        in_specs=[vmem(), vmem(), smem(), smem(), smem(), vmem(), vmem(), vmem()],
        out_specs=vmem(),
        scratch_shapes=[
            pltpu.VMEM((FRAMED, COLS), F32),
            pltpu.VMEM((STAMPS, WIN, 128), BF16),
            pltpu.VMEM((STAMPS, WIN, LANES), BF16),
            pltpu.VMEM((STAMPS * 32, LANES), BF16),
        ],
        compiler_params=params(16),
        name="stamp_sums",
    )(image, near, sigma, srow, scol, table, down, sky)


def fill_cols(wide, blocks):
    for i in range(4):
        for o in range(4):
            if abs(i - o) <= 1:
                wide[128 * i : 128 * i + 128, 128 * o : 128 * o + 128] = blocks[i - o + 1]
            else:
                wide[128 * i : 128 * i + 128, 128 * o : 128 * o + 128] = jnp.zeros((128, 128), BF16)


def across_body(image, near, blocks, out, framed, wide, border, held, sems):
    frame(framed, image, near)
    for m in range(0, FRAMED, 352):
        for v in range(3):
            border[v, m : m + 352] = jnp.dot(
                framed[m : m + 352, 128:384],
                jnp.concatenate([blocks[BASIS, v], blocks[BASIS + 1, v]], axis=0),
                preferred_element_type=F32,
            )
    lane = iota((352, 128), 1)

    def save(b, g):
        return pltpu.make_async_copy(held.at[g], out.at[b], sems.at[g])

    def four(v, c):
        for g in range(4):
            b = 4 * v + g
            for i in range(2):
                for o in range(2):
                    wide[128 * i : 128 * i + 128, 128 * o : 128 * o + 128] = blocks[b, i - o + 1]

            @pl.when(v > 0)
            def _():
                save(b - 4, g).wait()

            for m in range(0, FRAMED, 352):
                rows = slice(m, m + 352)
                left = jnp.dot(framed[rows, :256], wide[...], preferred_element_type=F32)
                right = jnp.dot(framed[rows, 256:], wide[...], preferred_element_type=F32)
                extra = border[v, rows]
                if g:
                    extra = pltpu.roll(extra, 128 - 32 * g, 1)
                held[g, rows, :128] = left[:, :128].astype(BF16)
                held[g, rows, 128:256] = (
                    left[:, 128:] + jnp.where(lane >= 118, extra, 0.0)
                ).astype(BF16)
                held[g, rows, 256:384] = (
                    right[:, :128] + jnp.where(lane < 10, extra, 0.0)
                ).astype(BF16)
                held[g, rows, 384:] = right[:, 128:].astype(BF16)
            save(b, g).start()
        return c

    lax.fori_loop(0, BASIS // 4, four, 0)
    for g in range(4):
        save(BASIS - 4 + g, g).wait()


def across_all(image, near, blocks):
    return pl.pallas_call(
        across_body,
        out_shape=shape((BASIS, FRAMED, COLS), BF16),
        in_specs=[vmem()] * 3,
        out_specs=hbm(),
        scratch_shapes=[
            pltpu.VMEM((FRAMED, COLS), BF16),
            pltpu.VMEM((256, 256), BF16),
            pltpu.VMEM((3, FRAMED, 128), F32),
            pltpu.VMEM((4, FRAMED, COLS), BF16),
            pltpu.SemaphoreType.DMA((4,)),
        ],
        compiler_params=params(50),
        cost_estimate=cost(BASIS * FRAMED * COLS * COLS, 16 * 10**6),
        name="across",
    )(image, near, blocks)


def solve(sums):
    total = jnp.sum(sums[...], axis=0)
    row, col = iota((16, 128), 0), iota((16, 128), 1)
    both = jnp.where(row < 8, total[0:1], total[1:2])
    both = jnp.where((col >> 4) == (row & 7), both, 0.0)
    for turn in (64, 32, 16):
        both = both + pltpu.roll(both, turn, 1)
    for k in range(BASIS):
        pivot = both[k : k + 1] / both[k : k + 1, k : k + 1]
        both = jnp.where(row == k, pivot, both - both[:, k : k + 1] * pivot)
    return both[:, BASIS : BASIS + 1]


def difference_body(
    across_in, sums_in, sigma_in, slot_in, table_in, science_in, coef_out, diff_out, leave_out,
    across, table, science, sums, sigma, slot, coef, bands, sems, load_sems, sky_sems, save_sems,
):
    ends = [0] + [first + span for first, _, span in BLOCKS]

    def load(i):
        some = pl.ds(ends[i], ends[i + 1] - ends[i])
        return pltpu.make_async_copy(
            across_in.at[:, some, :], across.at[:, some, :], load_sems.at[i]
        )

    small = [
        pltpu.make_async_copy(src, dst, sems.at[i])
        for i, (src, dst) in enumerate([(sums_in, sums), (sigma_in, sigma), (slot_in, slot)])
    ]
    table_load = pltpu.make_async_copy(table_in, table, sems.at[3])

    def sky_load(i):
        some = pl.ds(BLOCKS[i][0], BLOCKS[i][1])
        return pltpu.make_async_copy(science_in.at[some], science.at[some], sky_sems.at[i])

    def ahead(i):
        if i < len(BLOCKS):
            load(i).start()
            sky_load(i).start()

    for one in small:
        one.start()
    load(0).start()
    table_load.start()
    for one in small:
        one.wait()
    found = solve(sums)
    coef[...] = jnp.broadcast_to(found, coef.shape)
    eye = iota((16, 128), 0) == iota((16, 128), 1)
    coef_out[...] = jnp.sum(jnp.where(eye, found, 0.0), axis=0, keepdims=True)
    sky_load(0).start()
    for i in range(1, 2):
        ahead(i)
    scale = 1.0 / sigma[0]
    saves = []
    for i, (first, rows, span) in enumerate(BLOCKS):
        load(i).wait()
        ahead(i + 2)
        if i == 0:
            table_load.wait()
        for h in range(0, COLS, 256):
            model = None
            for b in range(BASIS):
                basis = jnp.dot(
                    table[b, :rows, :span],
                    across[b, first : first + span, h : h + 256],
                    preferred_element_type=F32,
                )
                term = coef[b : b + 1, :] * basis.astype(BF16).astype(F32)
                model = term if model is None else model + term
            if h == 0:
                sky_load(i).wait()
            left = (science[first : first + rows, h : h + 256] - model) * scale
            bands[first // 8 : (first + rows) // 8, :, h : h + 256] = left.reshape(
                rows // 8, 8, 256
            ).astype(BF16)

        def send(band, c):
            pltpu.make_async_copy(
                bands.at[band], leave_out.at[slot[band]], save_sems.at[0]
            ).start()
            return c

        lax.fori_loop(first // 8, (first + rows) // 8, send, 0, unroll=4)
        some = pl.ds(first // 8, rows // 8)
        saves.append(pltpu.make_async_copy(bands.at[some], diff_out.at[some], save_sems.at[1 + i]))
        saves[-1].start()
    for save in saves:
        save.wait()
    pltpu.make_async_copy(bands, leave_out.at[pl.ds(0, ROWS // 8)], save_sems.at[0]).wait()


def difference_all(sums, across, table, science, sigma, slot, slots):
    return pl.pallas_call(
        difference_body,
        out_shape=(
            shape((1, 128), F32),
            shape((ROWS // 8, 8, COLS), BF16),
            shape((slots, 8, COLS), BF16),
        ),
        in_specs=[hbm()] * 6,
        out_specs=(vmem(), hbm(), hbm()),
        scratch_shapes=[
            pltpu.VMEM((BASIS, FRAMED, COLS), BF16),
            pltpu.VMEM(table.shape, BF16),
            pltpu.VMEM(science.shape, F32),
            pltpu.VMEM(sums.shape, F32),
            pltpu.SMEM((1,), F32),
            pltpu.SMEM(slot.shape, I32),
            pltpu.VMEM((16, 256), F32),
            pltpu.VMEM((ROWS // 8, 8, COLS), BF16),
            pltpu.SemaphoreType.DMA((4,)),
            pltpu.SemaphoreType.DMA((len(BLOCKS),)),
            pltpu.SemaphoreType.DMA((len(BLOCKS),)),
            pltpu.SemaphoreType.DMA((1 + len(BLOCKS),)),
        ],
        compiler_params=params(53),
        name="difference",
    )(across, sums, sigma, slot, table, science)


def cut_body(diff, srow, scol, out, wide):
    wide[...] = diff[...].astype(F32).reshape(ROWS, COLS)
    row, lane = iota((32, 128), 0), iota((32, 128), 1)
    pick = (iota((8, 32), 1) >> 2 == iota((8, 32), 0)).astype(BF16)

    def cut(s, c):
        block = jnp.where(lane < 32, window(wide, srow[s], 32, scol[s]), 0.0)
        block = block + pltpu.roll(block, 32, 1)
        block = block + pltpu.roll(block, 64, 1)
        block = jnp.where((lane >> 5) == (row & 3), block, 0.0).astype(BF16)
        out[s] = jnp.dot(pick, block, preferred_element_type=F32).astype(BF16)
        return c

    lax.fori_loop(0, STAMPS, cut, 0)


def cut_stamps(diff, srow, scol):
    return pl.pallas_call(
        cut_body,
        out_shape=shape((STAMPS, 8, 128), BF16),
        in_specs=[vmem(), smem(), smem()],
        out_specs=vmem(),
        scratch_shapes=[pltpu.VMEM((ROWS, COLS), F32)],
        compiler_params=params(16),
        cost_estimate=cost(10**8, 3 * 10**6),
        name="cut_stamps",
    )(diff, srow, scol)


def smooth_body(landed, pick, blocks, out, patch, wide):
    fill_cols(wide, blocks)
    for first in range(0, ROWS, 256):

        def gather(m, c):
            pair = jnp.concatenate(
                [landed[pick[2 * m]].astype(F32), landed[pick[2 * m + 1]].astype(F32)], axis=0
            )
            patch[pl.ds(pl.multiple_of(m * 16, 16), 16)] = pair.astype(BF16)
            return c

        lax.fori_loop(first // 16, first // 16 + 16, gather, 0, unroll=4)
        out[first : first + 256] = jnp.dot(
            patch[first : first + 256], wide[...], preferred_element_type=F32
        ).astype(BF16)


def smooth(landed, pick, blocks):
    return pl.pallas_call(
        smooth_body,
        out_shape=shape((ROWS, COLS), BF16),
        in_specs=[vmem(), smem(), vmem()],
        out_specs=vmem(),
        scratch_shapes=[pltpu.VMEM((ROWS, COLS), BF16), pltpu.VMEM((COLS, COLS), BF16)],
        compiler_params=params(16),
        cost_estimate=cost(2 * ROWS * COLS * COLS, 3 * 10**6),
        name="smooth",
    )(landed, pick, blocks)


def fill_rows(table, blocks):
    table[:128, :128] = blocks[0]
    table[:128, 128:] = blocks[1]
    table[128:, :128] = jnp.zeros((STEP - 128, 128), BF16)
    table[128:, 128:] = blocks[0][: STEP - 128]


def filter_body(smoothed, near, cblocks, rblocks, out, framed, wide, table, tail, held, sems):
    fill_cols(wide, cblocks)
    fill_rows(table, rblocks)
    tail[...] = jnp.concatenate(
        [near[...].astype(F32), jnp.zeros((8, COLS), F32)], axis=0
    ).astype(BF16)
    edge = jnp.dot(tail[...], wide[...], preferred_element_type=F32)
    edge = jnp.where(lax.axis_index("strip") == 0, edge, jnp.concatenate([edge[8:], edge[:8]], axis=0))
    frame(framed, smoothed, edge.astype(BF16))
    saves = []
    for first, rows, span in BLOCKS:
        held[first : first + rows] = jnp.dot(
            table[:rows, :span], framed[first : first + span], preferred_element_type=F32
        )
        some = pl.ds(first, rows)
        saves.append(pltpu.make_async_copy(held.at[some], out.at[some], sems.at[len(saves)]))
        saves[-1].start()
    for save in saves:
        save.wait()


def filter_rows(smoothed, near, cblocks, rblocks):
    return pl.pallas_call(
        filter_body,
        out_shape=shape((ROWS, COLS), F32),
        in_specs=[vmem()] * 4,
        out_specs=hbm(),
        scratch_shapes=[
            pltpu.VMEM((FRAMED, COLS), BF16),
            pltpu.VMEM((COLS, COLS), BF16),
            pltpu.VMEM((STEP, SPAN), BF16),
            pltpu.VMEM((PAD, COLS), BF16),
            pltpu.VMEM((ROWS, COLS), F32),
            pltpu.SemaphoreType.DMA((len(BLOCKS),)),
        ],
        compiler_params=params(16),
        name="filter_rows",
    )(smoothed, near, cblocks, rblocks)


def shards(
    template, route_dest, route_row, kern_row, kern_col, science, noise_sigma,
    stamp_row, stamp_col, band_shift, psf_row, psf_col,
):
    ccds = lax.axis_size("ccd")
    devices = ccds * lax.axis_size("strip")
    bands = band_shift.shape[0]
    cap = 2 * bands // ccds
    outgoing = pack(route_dest, route_row, template, devices)
    arrived = lax.all_to_all(outgoing, BOTH, split_axis=0, concat_axis=0, tiled=True)
    cols, rows, pcols, prows, stamp_table, ready, down, slot, pick, sky = tables(
        kern_row, kern_col, psf_row, psf_col, band_shift, stamp_row, stamp_col, science
    )
    image, edge = coadd(arrived, ready)
    near = lax.ppermute(edge, "strip", SWAP)
    sums = stamp_sums(
        image, near, noise_sigma, stamp_row, stamp_col, stamp_table, down, sky, devices
    )
    sums = lax.all_to_all(sums, BOTH, split_axis=0, concat_axis=0, tiled=True)
    across = across_all(image, near, cols)
    coef, diff, leaving = difference_all(
        sums, across, rows, science, noise_sigma, slot, ccds * cap
    )
    landed = lax.all_to_all(
        leaving.reshape(ccds, cap, 8, COLS), "ccd", split_axis=0, concat_axis=0, tiled=True
    ).reshape(ccds * cap, 8, COLS)
    stamp_cut = cut_stamps(diff, stamp_row, stamp_col).reshape(STAMPS, 1024)
    last = jnp.where(lax.axis_index("strip") == 0, pick[bands - 1], pick[0])
    beside = lax.ppermute(
        lax.dynamic_slice(landed, (last, 0, 0), (1, 8, COLS))[0], "strip", SWAP
    )
    smoothed = smooth(landed, pick, pcols)
    filtered = filter_rows(smoothed, beside, pcols, prows)
    return (diff.reshape(ROWS, COLS), stamp_cut, coef[0, :BASIS], filtered)


def solution(mesh):
    placed = (
        P(BOTH, None, None), P(BOTH), P(BOTH), P(), P(), P(BOTH, None),
        P(BOTH), P(BOTH), P(BOTH), P(), P(), P(),
    )
    return jax.shard_map(
        shards,
        mesh=mesh,
        in_specs=placed,
        out_specs=(P(BOTH, None), P(BOTH, None), P(), P(BOTH, None)),
        check_vma=False,
    )
```
